256 devices in a mesh: user: 16 (over y, z_lo, core), item: 16 (over z_hi, x).
Axes of the slice: x: 4, y: 4, z: 8 (z_hi: 4, z_lo: 2; z = z_hi * 2 + z_lo), core: 2. Of those that a mesh axis runs over, the one named last changes fastest.
Arguments:
- user_states: bfloat16 [8192, 256], P('user'), may hold values from -240 to 240
- quot_rows: bfloat16 [16384, 256], P('item'), may hold values from -6 to 6
- rem_table: bfloat16 [4096, 256], replicated, may hold values from -6 to 6
- neg_rem: int32 [16384], P('item'), may hold values from 0 to 4095
- pos_quot: int32 [8192], P('user'), may hold values from 0 to 16383
- pos_rem: int32 [8192], P('user'), may hold values from 0 to 4095
Outputs:
- grad_users: float32 [8192, 256], P('user')
- grad_quot: float32 [16384, 256], P('item')
- grad_rem: float32 [4096, 256], replicated
The draws below stay inside these ranges and needn't reach their ends.
All inputs are finite; a program needn't handle non-finite values.
Results may differ from the reference program's by a relative error of at most 0.0065.
The reference program's roundings to bfloat16 on the way (of `neg_emb`, `pos_emb` and `probs`) count: a program that leaves them out, or rounds other values in their place, can miss the bound.
Values sent between devices are 32-bit elements; how exact they have to be, the bound alone decides.
A program may use at most 64 MiB of HBM per device.

```python
import jax
import jax.numpy as jnp
from jax import lax

D = 256
RROWS = 4096
USERS = 8192
NEG = 16384


def draw_user_states(key, part):
    key = jax.random.fold_in(key, 1)
    first = jax.random.fold_in(key, 0)
    values = jnp.clip(jax.random.normal(first, (USERS, D), jnp.float32), -6.0, 6.0)
    return values.astype(jnp.bfloat16)


def touch_ends(drawn, stream_key, least, top_value):
    shape = drawn.shape
    index_at = [jax.random.randint(jax.random.fold_in(stream_key, axis), (), 0, shape[axis]) for axis in range(len(shape))]
    drawn = drawn.at[tuple(index_at)].set(least)
    longest = shape.index(max(shape))
    index_at[longest] = (index_at[longest] + 1) % shape[longest]
    return drawn.at[tuple(index_at)].set(top_value)


def level_of(own_key, extent, shards, low, largest):
    loudness, own = 1.0, jax.random.fold_in(own_key, 6)
    for dim, blocks in shards:
        draws = jnp.exp(jax.random.uniform(jax.random.fold_in(own, dim), (blocks,), jnp.float32, low / len(shards), largest / len(shards)))
        loudness = loudness * jnp.repeat(draws, extent[dim] // blocks).reshape([-1 if axis == dim else 1 for axis in range(len(extent))])
    return loudness


def noise(stream_key, shape, scale, limit, shards=(), held_as=jnp.bfloat16):
    level = level_of(stream_key, shape, shards, -0.22, 0.18) if shards else 1.0
    array = jax.random.normal(stream_key, shape, jnp.float32) * scale * level
    return jnp.minimum(jnp.maximum(array, -limit), limit).astype(held_as)


def setup_inputs(seed: int = 0) -> dict:
    streams_of = jax.random.split(jax.random.key(seed), 7)
    user_states = draw_user_states(jax.random.fold_in(streams_of[6], 71), 0)
    quot_rows = noise(streams_of[1], (NEG, D), 1.0, 6.0, ((0, 16),))
    rem_table = noise(streams_of[2], (RROWS, D), 1.0, 6.0)
    neg_rem = touch_ends(jax.random.randint(streams_of[3], (NEG,), 0, RROWS), jax.random.fold_in(streams_of[3], 1), 0, RROWS - 1).astype(jnp.int32)
    pos_quot = touch_ends(jax.random.randint(streams_of[4], (USERS,), 0, NEG), jax.random.fold_in(streams_of[4], 1), 0, NEG - 1).astype(jnp.int32)
    pos_rem = touch_ends(jax.random.randint(streams_of[5], (USERS,), 0, RROWS), jax.random.fold_in(streams_of[5], 1), 0, RROWS - 1).astype(jnp.int32)
    return {"user_states": user_states, "quot_rows": quot_rows, "rem_table": rem_table, "neg_rem": neg_rem, "pos_quot": pos_quot, "pos_rem": pos_rem}


def reference(user_states, quot_rows, rem_table, neg_rem, pos_quot, pos_rem):
    f32 = jnp.float32
    scale = D ** -0.5
    rem_neg = rem_table[neg_rem]
    neg_emb = (quot_rows.astype(f32) * rem_neg.astype(f32)).astype(jnp.bfloat16)
    quot_pos = quot_rows[pos_quot]
    rem_pos = rem_table[pos_rem]
    pos_emb = (quot_pos.astype(f32) * rem_pos.astype(f32)).astype(jnp.bfloat16)
    pos_score = scale * jnp.sum(user_states.astype(f32) * pos_emb.astype(f32), axis=1)
    width = min(2048, NEG)
    blocks = neg_emb.reshape(NEG // width, width, D)

    def score(block):
        return scale * lax.dot_general(user_states, block, (((1,), (1,)), ((), ())), preferred_element_type=f32)

    top_neg = jnp.max(lax.map(lambda b: jnp.max(score(b), axis=1), blocks), axis=0)
    total = jnp.sum(lax.map(lambda b: jnp.sum(jnp.exp(score(b) - top_neg[:, None]), axis=1), blocks), axis=0)
    top = jnp.maximum(top_neg, pos_score)
    lse = top + jnp.log(total * jnp.exp(top_neg - top) + jnp.exp(pos_score - top))
    coef = scale * (jnp.exp(pos_score - lse) - 1.0)

    def backward(carry, block):
        probs = jnp.exp(score(block) - lse[:, None]).astype(jnp.bfloat16)
        carry = carry + scale * jnp.dot(probs, block, preferred_element_type=f32)
        grad_block = scale * lax.dot_general(probs, user_states, (((0,), (0,)), ((), ())), preferred_element_type=f32)
        return carry, grad_block

    grad_users, grad_blocks = lax.scan(backward, jnp.zeros((USERS, D), f32), blocks)
    grad_users = grad_users + coef[:, None] * pos_emb.astype(f32)
    grad_neg = grad_blocks.reshape(NEG, D)
    grad_pos = coef[:, None] * user_states.astype(f32)
    grad_quot = grad_neg * rem_neg.astype(f32)
    grad_quot = grad_quot.at[pos_quot].add(grad_pos * rem_pos.astype(f32))
    grad_rem = jax.ops.segment_sum(grad_neg * quot_rows.astype(f32), neg_rem, RROWS)
    grad_rem = grad_rem + jax.ops.segment_sum(grad_pos * quot_pos.astype(f32), pos_rem, RROWS)
    return grad_users, grad_quot, grad_rem
```

```python
import functools

import jax
import jax.numpy as jnp
from jax import lax
from jax.experimental import pallas as pl
from jax.experimental.pallas import tpu as pltpu
from jax.sharding import PartitionSpec as P

F32 = jnp.float32
BF16 = jnp.bfloat16
MESH = pl.DeviceIdType.MESH
D = 256
H = 128
NU = 512
NN = 1024
NR = 4096
SCALE = D ** (-0.5)


def coords():
    u = lax.axis_index("user")
    t = lax.axis_index("item")
    return t % 4, u // 4, (t // 4) * 2 + (u // 2) % 2, u % 2


def device(x, y, z, c):
    return (y * 4 + (z % 2) * 2 + c, (z // 2) * 4 + x)


def split_pair(v):
    hi = v.astype(BF16)
    lo = (v - hi.astype(F32)).astype(BF16)
    return hi, lo


def columns_of(row):
    return jnp.transpose(jnp.broadcast_to(row, (128, 128)))


def kernel(
    user, quot, rem, neg_rem, pos_quot, pos_rem,
    out_u, out_q, out_r,
    remneg, emb, rempos, qpos, pemb, st, pt, stat, stat_in, idx, idx_in, half, half_in,
    rhs, rhsq, gr, gq, gu, a1, a2, a3, b1, b2, b3, q1, q2, u1, u2,
    send, recv,
):
    x, y, z, c = coords()
    zh, zl = z // 2, z % 2
    t = zh * 4 + x
    sems = [0]

    def peer(dx=0, dy=0, dz=0, dc=0):
        return device((x + dx) % 4, (y + dy) % 4, (z + dz) % 8, (c + dc) % 2)

    def copy(src, dst, to):
        s = sems[0]
        sems[0] += 1
        return pltpu.make_async_remote_copy(
            src_ref=src, dst_ref=dst, send_sem=send.at[s], recv_sem=recv.at[s],
            device_id=to, device_id_type=MESH,
        )

    item_peers = [(dx, 0, dz, 0) for dz in (0, 2, 4, 6) for dx in range(4) if (dx, dz) != (0, 0)]
    z_peers = [(0, 0, dz, 0) for dz in (1, 3, 5, 7)]
    y_peers = [(0, dy, 0, 0) for dy in (1, 2, 3)]
    peers = item_peers + z_peers + y_peers + [(0, 0, 0, 1)]
    barrier = pltpu.get_barrier_semaphore()
    for p in peers:
        pl.semaphore_signal(barrier, inc=1, device_id=peer(*p), device_id_type=MESH)

    lanes_r = lax.broadcasted_iota(jnp.int32, (256, NR), 1).astype(F32)
    lanes_q = lax.broadcasted_iota(jnp.int32, (256, NN), 1).astype(F32)

    def picks(row_ref, first, shift, lanes):
        parts = []
        for k in range(2):
            at = pl.ds(pl.multiple_of(first + k * 128, 128), 128)
            parts.append(columns_of((row_ref[0:1, at] - shift).astype(F32)))
        col = jnp.concatenate(parts, axis=0)
        wide = jnp.concatenate([col] * (lanes.shape[1] // 128), axis=1)
        return jnp.where(wide == lanes, 1.0, 0.0).astype(BF16)

    def gather_neg(b, carry):
        r0 = pl.multiple_of(b * 256, 256)
        got = jnp.dot(picks(neg_rem, r0, 0, lanes_r), rem[...], preferred_element_type=F32)
        remneg[pl.ds(r0, 256), :] = got
        emb[pl.ds(r0, 256), :] = (quot[pl.ds(r0, 256), :].astype(F32) * got).astype(BF16)
        return carry

    lax.fori_loop(0, NN // 256, gather_neg, 0)
    first = t * NN

    def gather_pos(b, carry):
        r0 = pl.multiple_of(b * 256, 256)
        got_r = jnp.dot(picks(pos_rem, r0, 0, lanes_r), rem[...], preferred_element_type=F32)
        got_q = jnp.dot(picks(pos_quot, r0, first, lanes_q), quot[...], preferred_element_type=F32)
        rempos[pl.ds(r0, 256), :] = got_r
        qpos[pl.ds(r0, 256), :] = got_q
        pemb[pl.ds(r0, 256), :] = (got_q * got_r).astype(BF16).astype(F32)
        return carry

    lax.fori_loop(0, NU // 256, gather_pos, 0)
    idx[0:1, :] = pos_rem[...].astype(F32)
    idx[1:2, :] = (pos_quot[...] - first).astype(F32)

    def scores(b, top):
        r0 = pl.multiple_of(b * 256, 256)
        s = SCALE * lax.dot_general(
            emb[pl.ds(r0, 256), :], user[...], (((1,), (1,)), ((), ())), preferred_element_type=F32
        )
        st[pl.ds(r0, 256), :] = s
        return jnp.maximum(top, jnp.max(s.reshape(32, 8, NU), axis=0))

    top8 = lax.fori_loop(0, NN // 256, scores, jnp.full((8, NU), -jnp.inf, F32))
    top_row = jnp.max(top8, axis=0, keepdims=True)

    def totals(b, tot):
        r0 = pl.multiple_of(b * 256, 256)
        e = jnp.exp(st[pl.ds(r0, 256), :] - top_row)
        return tot + jnp.sum(e.reshape(32, 8, NU), axis=0)

    tot8 = lax.fori_loop(0, NN // 256, totals, jnp.zeros((8, NU), F32))
    tot_row = jnp.sum(tot8, axis=0, keepdims=True)
    for k in range(4):
        at = slice(k * 128, (k + 1) * 128)
        stat[k : k + 1, :] = top_row[:, at]
        stat[4 + k : 5 + k, :] = tot_row[:, at]
        prod = user[at, :].astype(F32) * pemb[at, :]
        prod = prod[:, :H] + prod[:, H:]
        stat[8 + k : 9 + k, :] = SCALE * jnp.sum(jnp.transpose(prod), axis=0, keepdims=True)

    pl.semaphore_wait(barrier, len(peers))
    stat_copies = [copy(stat, stat_in.at[n], peer(*p)) for n, p in enumerate(item_peers)]
    for cp in stat_copies:
        cp.start()
    idx_copy = copy(idx, idx_in, peer(dc=1))
    idx_copy.start()
    for cp in stat_copies:
        cp.wait_recv()
    tops = [stat[0:4, :]] + [stat_in[n, 0:4, :] for n in range(15)]
    top_neg = functools.reduce(jnp.maximum, tops)
    total = stat[4:8, :] * jnp.exp(tops[0] - top_neg)
    pos_score = stat[8:12, :]
    for n in range(15):
        total = total + stat_in[n, 4:8, :] * jnp.exp(tops[n + 1] - top_neg)
        pos_score = pos_score + stat_in[n, 8:12, :]
    top = jnp.maximum(top_neg, pos_score)
    lse = top + jnp.log(total * jnp.exp(top_neg - top) + jnp.exp(pos_score - top))
    coef = SCALE * (jnp.exp(pos_score - lse) - 1.0)
    lse_row = jnp.concatenate([lse[k : k + 1, :] for k in range(4)], axis=1)

    def backward(b, carry):
        r0 = pl.multiple_of(b * 256, 256)
        at = pl.ds(r0, 256)
        p = jnp.exp(st[at, :] - lse_row).astype(BF16)
        pt[at, :] = p
        g = SCALE * jnp.dot(p, user[...], preferred_element_type=F32)
        half[0, at, :] = g[:, :H]
        half[1, at, :] = g[:, H:]
        return carry

    lax.fori_loop(0, NN // 256, backward, 0)
    for k in range(4):
        at = slice(k * 128, (k + 1) * 128)
        col = columns_of(coef[k : k + 1, :])
        for h in range(2):
            cols = slice(h * H, (h + 1) * H)
            gp = col * user[at, cols].astype(F32)
            owned = jnp.where(idx_col_owned(idx, k), gp, 0.0)
            half[h, NN + k * 128 : NN + (k + 1) * 128, :] = owned * qpos[at, cols]
            half[h, NN + NU + k * 128 : NN + NU + (k + 1) * 128, :] = owned * rempos[at, cols]
            gu[at, cols] = col * pemb[at, cols]
    half_copy = copy(half.at[1 - c], half_in, peer(dc=1))
    half_copy.start()

    def users(b, carry):
        at = pl.ds(pl.multiple_of(b * 256, 256), 256)
        g = lax.dot_general(
            pt[at, :], emb[at, :], (((0,), (0,)), ((), ())), preferred_element_type=F32
        )
        gu[...] += SCALE * g
        return carry

    lax.fori_loop(0, NN // 256, users, 0)

    def rows(first_row, count):
        return pl.ds(pl.multiple_of(first_row, 8), count)

    u_x = []
    for d in (1, 3, 2):
        cp = copy(gu.at[rows(((x + d) % 4) * 128, 128)], u1.at[d - 1], peer(dx=d))
        cp.start()
        u_x.append(cp)

    idx_copy.wait()
    half_copy.wait_recv()
    first_half = c == 0

    def pair(b, carry):
        at = pl.ds(pl.multiple_of(b * 256, 256), 256)
        g = half[c, at, :] + half_in[at, :]
        q = jnp.where(first_half, quot[at, :H].astype(F32), quot[at, H:].astype(F32))
        hi, lo = split_pair(g * q)
        rhs[at, :H] = hi
        rhs[at, H:] = lo
        rn = jnp.where(first_half, remneg[at, :H], remneg[at, H:])
        gq[at, :] = g * rn
        return carry

    lax.fori_loop(0, NN // 256, pair, 0)
    for base, src in ((0, half.at[c]), (NU, half_in)):
        hi, lo = split_pair(src[NN : NN + NU, :])
        rhs[NN + base : NN + base + NU, :H] = hi
        rhs[NN + base : NN + base + NU, H:] = lo
        hi, lo = split_pair(src[NN + NU : NN + 2 * NU, :])
        rhsq[base : base + NU, :H] = hi
        rhsq[base : base + NU, H:] = lo

    slots = jnp.concatenate([idx[1:2, :], idx_in[1:2, :]], axis=1)
    down_q = lax.broadcasted_iota(jnp.int32, (256, 2 * NU), 0).astype(F32)
    q_y = {}
    for d in (2, 1, 3, 0):
        r0 = ((y + d) % 4) * 256
        at = rows(r0, 256)
        pick = jnp.where(down_q + lax.convert_element_type(r0, F32) == slots, 1.0, 0.0).astype(BF16)
        g = jnp.dot(pick, rhsq[...], preferred_element_type=F32)
        gq[at, :] += g[:, :H] + g[:, H:]
        if d:
            q_y[d] = copy(gq.at[at], q1.at[d - 1], peer(dy=d))
            q_y[d].start()

    which = jnp.concatenate([neg_rem[...].astype(F32), idx[0:1, :], idx_in[0:1, :]], axis=1)
    down_r = lax.broadcasted_iota(jnp.int32, (256, NN + 2 * NU), 0).astype(F32)

    def make(r0):
        def step(b, carry):
            at0 = r0 + b * 256
            shift = lax.convert_element_type(at0, F32)
            pick = jnp.where(down_r == which - shift, 1.0, 0.0).astype(BF16)
            g = jnp.dot(pick, rhs[...], preferred_element_type=F32)
            gr[pl.ds(pl.multiple_of(at0, 256), 256), :] = g[:, :H] + g[:, H:]
            return carry

        lax.fori_loop(0, 2, step, 0)

    a_x, b_y = {}, {}
    for d in (2, 1, 3, 0):
        ra = ((x + d) % 4) * 512
        make(ra)
        if d:
            a_x[d] = copy(gr.at[rows(ra, 512)], a1.at[d - 1], peer(dx=d))
            a_x[d].start()
        rb = 2048 + ((y + d) % 4) * 512
        make(rb)
        if d:
            b_y[d] = copy(gr.at[rows(rb, 512)], b1.at[d - 1], peer(dy=d))
            b_y[d].start()

    def reduce(dst, r0, count, slots_ref, copies, n):
        for cp in copies:
            cp.wait_recv()
        v = dst[rows(r0, count), :]
        for k in range(n):
            v = v + slots_ref[k]
        dst[rows(r0, count), :] = v

    def start_all(cps):
        for cp in cps:
            cp.start()
        return cps

    ru = x * 128
    reduce(gu, ru, 128, u1, u_x, 3)
    u_z = start_all([
        copy(gu.at[rows(ru + ((zh + d) % 4) * 32, 32)], u2.at[d - 1], peer(dz=2 * d)) for d in (1, 3, 2)
    ])
    rq = y * 256
    reduce(gq, rq, 256, q1, q_y.values(), 3)
    q_z = start_all([copy(gq.at[rows(rq + (1 - zl) * 128, 128)], q2.at[0], peer(dz=1 - 2 * zl))])

    ra, rb = x * 512, 2048 + y * 512
    reduce(gr, ra, 512, a1, a_x.values(), 3)
    a_y = start_all([
        copy(gr.at[rows(ra + ((y + d) % 4) * 128, 128)], a2.at[d - 1], peer(dy=d)) for d in (2, 1, 3)
    ])
    reduce(gr, rb, 512, b1, b_y.values(), 3)
    b_x = start_all([
        copy(gr.at[rows(rb + ((x + d) % 4) * 128, 128)], b2.at[d - 1], peer(dx=d)) for d in (2, 1, 3)
    ])

    ru2 = ru + zh * 32
    for cp in u_z:
        cp.wait_recv()
    out_u[rows(ru2, 32), :] = gu[rows(ru2, 32), :] + u2[0] + u2[1] + u2[2]
    u_bz = start_all([
        copy(out_u.at[rows(ru2, 32)], out_u.at[rows(ru2, 32)], peer(dz=2 * d)) for d in (1, 3, 2)
    ])
    rq2 = rq + zl * 128
    q_z[0].wait_recv()
    out_q[c, rows(rq2, 128), :] = gq[rows(rq2, 128), :] + q2[0]
    q_bz = start_all([
        copy(out_q.at[c, rows(rq2, 128)], out_q.at[c, rows(rq2, 128)], peer(dz=1 - 2 * zl))
    ])

    ra2, rb2 = ra + y * 128, rb + x * 128
    reduce(gr, ra2, 128, a2, a_y, 3)
    z_order = (4, 3, 5, 2, 6, 1, 7)
    a_z = start_all([
        copy(gr.at[rows(ra2 + ((z + d) % 8) * 16, 16)], a3.at[d - 1], peer(dz=d)) for d in z_order
    ])
    reduce(gr, rb2, 128, b2, b_x, 3)
    b_z = start_all([
        copy(gr.at[rows(rb2 + ((z + d) % 8) * 16, 16)], b3.at[d - 1], peer(dz=d)) for d in z_order
    ])

    for cp in u_bz:
        cp.wait_recv()
    u_bx = start_all([
        copy(out_u.at[rows(ru, 128)], out_u.at[rows(ru, 128)], peer(dx=d)) for d in (2, 1, 3)
    ])
    q_bz[0].wait_recv()
    q_by = start_all([
        copy(out_q.at[c, rows(rq, 256)], out_q.at[c, rows(rq, 256)], peer(dy=d)) for d in (2, 1, 3)
    ])
    q_c = start_all([copy(out_q.at[c, rows(rq, 256)], out_q.at[c, rows(rq, 256)], peer(dc=1))])

    def finish(copies, r0, slots_ref):
        for cp in copies:
            cp.wait_recv()
        v = gr[rows(r0, 16), :]
        for k in range(7):
            v = v + slots_ref[k]
        out_r[c, rows(r0, 16), :] = v
        return start_all([
            copy(out_r.at[c, rows(r0, 16)], out_r.at[c, rows(r0, 16)], peer(dz=d)) for d in z_order
        ])

    a_bz = finish(a_z, ra2 + z * 16, a3)
    b_bz = finish(b_z, rb2 + z * 16, b3)

    def back(r0, count, axis):
        at = rows(r0, count)
        sent = [
            copy(out_r.at[c, at], out_r.at[c, at], peer(**{axis: d})) for d in (2, 1, 3)
        ]
        start_all(sent)
        return sent

    def over(r0, count):
        at = rows(r0, count)
        return start_all([copy(out_r.at[c, at], out_r.at[c, at], peer(dc=1))])

    for cp in a_bz:
        cp.wait_recv()
    a_by = back(ra2, 128, "dy")
    for cp in b_bz:
        cp.wait_recv()
    b_bx = back(rb2, 128, "dx")
    pairs = over(ra2, 128) + over(rb2, 128)
    for cp in a_by:
        cp.wait_recv()
    a_bx = back(ra, 512, "dx")
    for cp in b_bx:
        cp.wait_recv()
    b_by = back(rb, 512, "dy")
    for d in (2, 1, 3):
        pairs += over(x * 512 + ((y - d) % 4) * 128, 128)
        pairs += over(2048 + y * 512 + ((x - d) % 4) * 128, 128)
    for d, cp in zip((2, 1, 3), q_by):
        cp.wait_recv()
        q_c += over_q(out_q, copy, peer, c, rows, ((y - d) % 4) * 256)
    for k in (1, 2, 0):
        d = (2, 1, 3)[k]
        a_bx[k].wait_recv()
        pairs += over(((x - d) % 4) * 512, 512)
        b_by[k].wait_recv()
        pairs += over(2048 + ((y - d) % 4) * 512, 512)
    for cp in u_bx:
        cp.wait_recv()
    for cp in q_c + pairs:
        cp.wait_recv()
    sent = stat_copies + [half_copy] + u_x + list(q_y.values()) + list(a_x.values()) + list(b_y.values())
    sent += u_z + q_z + a_y + b_x + u_bz + q_bz + a_z + b_z + u_bx + q_by + q_c
    sent += a_bz + b_bz + a_by + b_bx + a_bx + b_by + pairs
    for cp in sent:
        cp.wait_send()


def idx_col_owned(idx, k):
    col = columns_of(idx[1:2, k * 128 : (k + 1) * 128])
    return (col >= 0.0) & (col < float(NN))


def over_q(out_q, copy, peer, c, rows, r0):
    at = rows(r0, 256)
    cp = copy(out_q.at[c, at], out_q.at[c, at], peer(dc=1))
    cp.start()
    return [cp]


COPIES = 140


def per_device(user_states, quot_rows, rem_table, neg_rem, pos_quot, pos_rem):
    vmem = pl.BlockSpec(memory_space=pltpu.VMEM)
    out_u, out_q, out_r = pl.pallas_call(
        kernel,
        out_shape=(
            jax.ShapeDtypeStruct((NU, D), F32),
            jax.ShapeDtypeStruct((2, NN, H), F32),
            jax.ShapeDtypeStruct((2, NR, H), F32),
        ),
        in_specs=[vmem] * 6,
        out_specs=(vmem, vmem, vmem),
        scratch_shapes=[
            pltpu.VMEM((NN, D), F32),
            pltpu.VMEM((NN, D), BF16),
            pltpu.VMEM((NU, D), F32),
            pltpu.VMEM((NU, D), F32),
            pltpu.VMEM((NU, D), F32),
            pltpu.VMEM((NN, NU), F32),
            pltpu.VMEM((NN, NU), BF16),
            pltpu.VMEM((12, 128), F32),
            pltpu.VMEM((15, 12, 128), F32),
            pltpu.VMEM((2, NU), F32),
            pltpu.VMEM((2, NU), F32),
            pltpu.VMEM((2, NN + 2 * NU, H), F32),
            pltpu.VMEM((NN + 2 * NU, H), F32),
            pltpu.VMEM((NN + 2 * NU, D), BF16),
            pltpu.VMEM((2 * NU, D), BF16),
            pltpu.VMEM((NR, H), F32),
            pltpu.VMEM((NN, H), F32),
            pltpu.VMEM((NU, D), F32),
            pltpu.VMEM((3, 512, H), F32),
            pltpu.VMEM((3, 128, H), F32),
            pltpu.VMEM((7, 16, H), F32),
            pltpu.VMEM((3, 512, H), F32),
            pltpu.VMEM((3, 128, H), F32),
            pltpu.VMEM((7, 16, H), F32),
            pltpu.VMEM((3, 256, H), F32),
            pltpu.VMEM((1, 128, H), F32),
            pltpu.VMEM((3, 128, D), F32),
            pltpu.VMEM((3, 32, D), F32),
            pltpu.SemaphoreType.DMA((COPIES,)),
            pltpu.SemaphoreType.DMA((COPIES,)),
        ],
        compiler_params=pltpu.CompilerParams(
            collective_id=0, has_side_effects=True, vmem_limit_bytes=56 << 20
        ),
        cost_estimate=pl.CostEstimate(flops=12 << 30, bytes_accessed=9 << 20, transcendentals=1 << 20),
        name="sampled_softmax_grads",
    )(
        user_states, quot_rows, rem_table,
        neg_rem.reshape(1, NN), pos_quot.reshape(1, NU), pos_rem.reshape(1, NU),
    )
    grad_quot = jnp.swapaxes(out_q, 0, 1).reshape(NN, D)
    grad_rem = jnp.swapaxes(out_r, 0, 1).reshape(NR, D)
    return out_u, grad_quot, grad_rem


def solution(mesh):
    in_specs = (P("user", None), P("item", None), P(), P("item"), P("user"), P("user"))
    out_specs = (P("user", None), P("item", None), P())
    return jax.shard_map(
        per_device, mesh=mesh, in_specs=in_specs, out_specs=out_specs, check_vma=False
    )
```

```python
import functools

import jax
import jax.numpy as jnp
from jax import lax
from jax.experimental import pallas as pl
from jax.experimental.pallas import tpu as pltpu
from jax.sharding import PartitionSpec as P

F32 = jnp.float32
BF16 = jnp.bfloat16
MESH = pl.DeviceIdType.MESH
D = 256
H = 128
NU = 512
NN = 1024
NR = 4096
SCALE = D ** (-0.5)


def coords():
    u = lax.axis_index("user")
    t = lax.axis_index("item")
    return t % 4, u // 4, (t // 4) * 2 + (u // 2) % 2, u % 2


def device(x, y, z, c):
    return (y * 4 + (z % 2) * 2 + c, (z // 2) * 4 + x)


def split_pair(v):
    hi = v.astype(BF16)
    lo = (v - hi.astype(F32)).astype(BF16)
    return hi, lo


def columns_of(row):
    return jnp.transpose(jnp.broadcast_to(row, (128, 128)))


def kernel(
    user_hbm, quot_hbm, rem_hbm, neg_rem_hbm, pos_quot_hbm, pos_rem_hbm,
    out_u, out_q, out_r,
    user, quot, rem, neg_rem, pos_quot, pos_rem,
    remneg, emb, rempos, qpos, pemb, st, pt, stat, stat_in, idx, idx_in, half, half_in,
    rhs, rhsq, gr, gq, gu, first_in, second_in, third_in, q1, q2, u1, u2,
    load, send, recv,
):
    x, y, z, c = coords()
    zh, zl = z // 2, z % 2
    t = zh * 4 + x
    mine = pl.ds(pl.multiple_of(c * H, H), H)
    others = pl.ds(pl.multiple_of((1 - c) * H, H), H)

    def peer(dx=0, dy=0, dz=0, dc=0):
        return device((x + dx) % 4, (y + dy) % 4, (z + dz) % 8, (c + dc) % 2)

    item_peers = [(dx, 0, dz, 0) for dz in (0, 2, 4, 6) for dx in range(4) if (dx, dz) != (0, 0)]
    z_peers = [(0, 0, dz, 0) for dz in (1, 3, 5, 7)]
    y_peers = [(0, dy, 0, 0) for dy in (1, 2, 3)]
    peers = item_peers + z_peers + y_peers + [(0, 0, 0, 1)]
    barrier = pltpu.get_barrier_semaphore()
    for p in peers:
        pl.semaphore_signal(barrier, inc=1, device_id=peer(*p), device_id_type=MESH)

    loads = []
    for n, (src, dst) in enumerate((
        (neg_rem_hbm, neg_rem), (rem_hbm, rem), (quot_hbm, quot),
        (pos_rem_hbm, pos_rem), (pos_quot_hbm, pos_quot), (user_hbm, user),
    )):
        loads.append(pltpu.make_async_copy(src, dst, load.at[n]))
        loads[-1].start()

    sent = {}
    recvs = [0]

    def slot():
        recvs[0] += 1
        return recvs[0] - 1

    def go(src, dst, to, s, r, size):
        pltpu.make_async_remote_copy(
            src_ref=src, dst_ref=dst, send_sem=send.at[s], recv_sem=recv.at[r],
            device_id=to, device_id_type=MESH,
        ).start()
        sent[s] = sent.get(s, 0) + size

    def landed(ref, r):
        pltpu.make_async_remote_copy(
            src_ref=ref, dst_ref=ref, send_sem=send.at[0], recv_sem=recv.at[r],
            device_id=peer(dc=1), device_id_type=MESH,
        ).wait_recv()

    def left(ref, s):
        pltpu.make_async_remote_copy(
            src_ref=ref, dst_ref=ref, send_sem=send.at[s], recv_sem=recv.at[0],
            device_id=peer(dc=1), device_id_type=MESH,
        ).wait_send()

    def rows(first_row, count):
        return pl.ds(pl.multiple_of(first_row, 8), count)

    lanes_r = lax.broadcasted_iota(jnp.int32, (256, NR), 1).astype(F32)
    lanes_q = lax.broadcasted_iota(jnp.int32, (256, NN), 1).astype(F32)

    def picks(row_ref, first, shift, lanes):
        parts = []
        for k in range(2):
            at = pl.ds(pl.multiple_of(first + k * 128, 128), 128)
            parts.append(columns_of((row_ref[0:1, at] - shift).astype(F32)))
        col = jnp.concatenate(parts, axis=0)
        wide = jnp.concatenate([col] * (lanes.shape[1] // 128), axis=1)
        return jnp.where(wide == lanes, 1.0, 0.0).astype(BF16)

    def gather_neg(b, carry):
        r0 = pl.multiple_of(b * 256, 256)
        got = jnp.dot(picks(neg_rem, r0, 0, lanes_r), rem[...], preferred_element_type=F32)
        remneg[pl.ds(r0, 256), :] = got
        emb[pl.ds(r0, 256), :] = (quot[pl.ds(r0, 256), :].astype(F32) * got).astype(BF16)
        return carry

    for n in (0, 1, 2):
        loads[n].wait()
    lax.fori_loop(0, NN // 256, gather_neg, 0)
    first = t * NN

    def gather_pos(b, carry):
        r0 = pl.multiple_of(b * 256, 256)
        got_r = jnp.dot(picks(pos_rem, r0, 0, lanes_r), rem[...], preferred_element_type=F32)
        got_q = jnp.dot(picks(pos_quot, r0, first, lanes_q), quot[...], preferred_element_type=F32)
        rempos[pl.ds(r0, 256), :] = got_r
        qpos[pl.ds(r0, 256), :] = got_q
        pemb[pl.ds(r0, 256), :] = (got_q * got_r).astype(BF16).astype(F32)
        return carry

    for n in (3, 4, 5):
        loads[n].wait()
    lax.fori_loop(0, NU // 256, gather_pos, 0)
    idx[0:1, :] = pos_rem[...].astype(F32)
    idx[1:2, :] = (pos_quot[...] - first).astype(F32)

    def scores(b, top):
        r0 = pl.multiple_of(b * 256, 256)
        s = SCALE * lax.dot_general(
            emb[pl.ds(r0, 256), :], user[...], (((1,), (1,)), ((), ())), preferred_element_type=F32
        )
        st[pl.ds(r0, 256), :] = s
        return jnp.maximum(top, jnp.max(s.reshape(32, 8, NU), axis=0))

    top8 = lax.fori_loop(0, NN // 256, scores, jnp.full((8, NU), -jnp.inf, F32))
    top_row = jnp.max(top8, axis=0, keepdims=True)

    def totals(b, tot):
        r0 = pl.multiple_of(b * 256, 256)
        e = jnp.exp(st[pl.ds(r0, 256), :] - top_row)
        return tot + jnp.sum(e.reshape(32, 8, NU), axis=0)

    tot8 = lax.fori_loop(0, NN // 256, totals, jnp.zeros((8, NU), F32))
    tot_row = jnp.sum(tot8, axis=0, keepdims=True)
    for k in range(4):
        at = slice(k * 128, (k + 1) * 128)
        stat[k : k + 1, :] = top_row[:, at]
        stat[4 + k : 5 + k, :] = tot_row[:, at]
        prod = user[at, :].astype(F32) * pemb[at, :]
        prod = prod[:, :H] + prod[:, H:]
        stat[8 + k : 9 + k, :] = SCALE * jnp.sum(jnp.transpose(prod), axis=0, keepdims=True)

    pl.semaphore_wait(barrier, len(peers))
    r_stat, r_idx, r_half = slot(), slot(), slot()
    for n, p in enumerate(item_peers):
        go(stat, stat_in.at[n], peer(*p), 0, r_stat, 12)
    go(idx, idx_in, peer(dc=1), 1, r_idx, 8)
    landed(stat_in, r_stat)
    tops = [stat[0:4, :]] + [stat_in[n, 0:4, :] for n in range(15)]
    top_neg = functools.reduce(jnp.maximum, tops)
    total = stat[4:8, :] * jnp.exp(tops[0] - top_neg)
    pos_score = stat[8:12, :]
    for n in range(15):
        total = total + stat_in[n, 4:8, :] * jnp.exp(tops[n + 1] - top_neg)
        pos_score = pos_score + stat_in[n, 8:12, :]
    top = jnp.maximum(top_neg, pos_score)
    lse = top + jnp.log(total * jnp.exp(top_neg - top) + jnp.exp(pos_score - top))
    coef = SCALE * (jnp.exp(pos_score - lse) - 1.0)
    lse_row = jnp.concatenate([lse[k : k + 1, :] for k in range(4)], axis=1)

    def backward(b, carry):
        r0 = pl.multiple_of(b * 256, 256)
        at = pl.ds(r0, 256)
        p = jnp.exp(st[at, :] - lse_row).astype(BF16)
        pt[at, :] = p
        g = SCALE * jnp.dot(p, user[...], preferred_element_type=F32)
        half[0, at, :] = g[:, :H]
        half[1, at, :] = g[:, H:]
        return carry

    lax.fori_loop(0, NN // 256, backward, 0)
    for k in range(4):
        at = slice(k * 128, (k + 1) * 128)
        col = columns_of(coef[k : k + 1, :])
        slot_col = columns_of(idx[1:2, at])
        owned = (slot_col >= 0.0) & (slot_col < float(NN))
        for h in range(2):
            cols = slice(h * H, (h + 1) * H)
            gp = jnp.where(owned, col * user[at, cols].astype(F32), 0.0)
            half[h, NN + k * 128 : NN + (k + 1) * 128, :] = gp * qpos[at, cols]
            half[h, NN + NU + k * 128 : NN + NU + (k + 1) * 128, :] = gp * rempos[at, cols]
            gu[at, cols] = col * pemb[at, cols]
    go(half.at[1 - c], half_in, peer(dc=1), 2, r_half, NN + 2 * NU)

    def users(b, carry):
        at = pl.ds(pl.multiple_of(b * 256, 256), 256)
        g = lax.dot_general(
            pt[at, :], emb[at, :], (((0,), (0,)), ((), ())), preferred_element_type=F32
        )
        gu[...] += SCALE * g
        return carry

    lax.fori_loop(0, NN // 256, users, 0)
    r_ux = slot()
    for d in (1, 3, 2):
        go(gu.at[rows(((x + d) % 4) * 128, 128)], u1.at[d - 1], peer(dx=d), 3, r_ux, 256)

    landed(idx_in, r_idx)
    landed(half_in, r_half)
    first_half = c == 0

    def pair(b, carry):
        at = pl.ds(pl.multiple_of(b * 256, 256), 256)
        g = half[c, at, :] + half_in[at, :]
        q = jnp.where(first_half, quot[at, :H].astype(F32), quot[at, H:].astype(F32))
        hi, lo = split_pair(g * q)
        rhs[at, :H] = hi
        rhs[at, H:] = lo
        rn = jnp.where(first_half, remneg[at, :H], remneg[at, H:])
        gq[at, :] = g * rn
        return carry

    lax.fori_loop(0, NN // 256, pair, 0)
    for base, src in ((0, half.at[c]), (NU, half_in)):
        hi, lo = split_pair(src[NN : NN + NU, :])
        rhs[NN + base : NN + base + NU, :H] = hi
        rhs[NN + base : NN + base + NU, H:] = lo
        hi, lo = split_pair(src[NN + NU : NN + 2 * NU, :])
        rhsq[base : base + NU, :H] = hi
        rhsq[base : base + NU, H:] = lo

    slots = jnp.concatenate([idx[1:2, :], idx_in[1:2, :]], axis=1)
    down_q = lax.broadcasted_iota(jnp.int32, (256, 2 * NU), 0).astype(F32)
    r_qy = slot()
    for d in (2, 1, 3, 0):
        r0 = ((y + d) % 4) * 256
        at = rows(r0, 256)
        pick = jnp.where(down_q + lax.convert_element_type(r0, F32) == slots, 1.0, 0.0).astype(BF16)
        g = jnp.dot(pick, rhsq[...], preferred_element_type=F32)
        gq[at, :] += g[:, :H] + g[:, H:]
        if d:
            go(gq.at[at], q1.at[d - 1], peer(dy=d), 4, r_qy, 256)

    which = jnp.concatenate([neg_rem[...].astype(F32), idx[0:1, :], idx_in[0:1, :]], axis=1)
    down_r = lax.broadcasted_iota(jnp.int32, (256, NN + 2 * NU), 0).astype(F32)
    axes = {"x": x, "y": y}
    order = (2, 1, 3, 0)
    parts = [(0, "x", "y"), (1, "y", "x"), (2, "x", "y"), (3, "y", "x")]
    r_part = [{k: slot() for k in ("one", "two", "three", "z", "s1", "s2", "s3", "f1", "f2", "f3")} for _ in parts]
    r_pair = slot()

    def towards(axis, d):
        return peer(**{"d" + axis: d})

    def place(axis, d=0):
        return (axes[axis] + d) % 4

    def one(n, d):
        p, fst, snd = parts[n]
        r0 = p * 1024 + place(fst, d) * 256
        pick = jnp.where(down_r == which - lax.convert_element_type(r0, F32), 1.0, 0.0).astype(BF16)
        g = jnp.dot(pick, rhs[...], preferred_element_type=F32)
        gr[rows(r0, 256), :] = g[:, :H] + g[:, H:]
        if d:
            go(gr.at[rows(r0, 256)], first_in.at[n, d - 1], towards(fst, d), 5 + n, r_part[n]["one"], 256)

    def fold(dst, r0, count, slots_ref, n):
        v = dst[rows(r0, count), :]
        for k in range(n):
            v = v + slots_ref[k]
        return v

    def base1(n):
        p, fst, snd = parts[n]
        return p * 1024 + place(fst) * 256

    def base2(n):
        return base1(n) + place(parts[n][2]) * 64

    def base3(n):
        return base2(n) + z * 8

    def two(n):
        p, fst, snd = parts[n]
        landed(first_in.at[n], r_part[n]["one"])
        gr[rows(base1(n), 256), :] = fold(gr, base1(n), 256, first_in.at[n], 3)
        for d in (2, 1, 3):
            at = rows(base1(n) + place(snd, d) * 64, 64)
            go(gr.at[at], second_in.at[n, d - 1], towards(snd, d), 5 + n, r_part[n]["two"], 64)

    z_order = (4, 3, 5, 2, 6, 1, 7)

    def three(n):
        landed(second_in.at[n], r_part[n]["two"])
        gr[rows(base2(n), 64), :] = fold(gr, base2(n), 64, second_in.at[n], 3)
        for d in z_order:
            at = rows(base2(n) + ((z + d) % 8) * 8, 8)
            go(gr.at[at], third_in.at[n, d - 1], peer(dz=d), 5 + n, r_part[n]["three"], 8)

    def share(at, to, n, key, size):
        go(out_r.at[at, mine], out_r.at[at, mine], to, 9 + n, r_part[n][key], size)

    def back_z(n):
        landed(third_in.at[n], r_part[n]["three"])
        at = rows(base3(n), 8)
        out_r[at, mine] = fold(gr, base3(n), 8, third_in.at[n], 7)
        for d in z_order:
            share(at, peer(dz=d), n, "z", 8)

    def first_axis(n, at):
        for d in (2, 1, 3):
            share(at, towards(parts[n][1], d), n, f"f{d}", 64)

    def back_second(n):
        landed(out_r.at[0:56, mine], r_part[n]["z"])
        at = rows(base2(n), 64)
        first_axis(n, at)
        for d in (2, 1, 3):
            share(at, towards(parts[n][2], d), n, f"s{d}", 64)

    def back_first(n):
        for d in (1, 3, 2):
            at = rows(base1(n) + place(parts[n][2], -d) * 64, 64)
            landed(out_r.at[at, mine], r_part[n][f"s{d}"])
            first_axis(n, at)

    def to_pair(at):
        go(out_r.at[at, mine], out_r.at[at, mine], peer(dc=1), 13, r_pair, 256)

    def back_pair(n, d):
        p, fst, snd = parts[n]
        at = rows(p * 1024 + place(fst, -d) * 256, 256)
        if d:
            landed(out_r.at[at, mine], r_part[n][f"f{d}"])
        to_pair(at)

    for d in order:
        one(0, d)
        one(1, d)
    for d in order:
        one(2, d)
        one(3, d)

    ru = x * 128
    landed(u1, r_ux)
    gu[rows(ru, 128), :] = fold(gu, ru, 128, u1, 3)
    r_uz = slot()
    for d in (2, 1, 3):
        go(gu.at[rows(ru + ((zh + d) % 4) * 32, 32)], u2.at[d - 1], peer(dz=2 * d), 14, r_uz, 64)
    rq = y * 256
    landed(q1, r_qy)
    gq[rows(rq, 256), :] = fold(gq, rq, 256, q1, 3)
    r_qz = slot()
    go(gq.at[rows(rq + (1 - zl) * 128, 128)], q2.at[0], peer(dz=1 - 2 * zl), 15, r_qz, 128)

    two(0)
    two(1)
    ru2 = ru + zh * 32
    landed(u2, r_uz)
    out_u[rows(ru2, 32), :] = fold(gu, ru2, 32, u2, 3)
    r_ubz = slot()
    for d in (2, 1, 3):
        at = rows(ru2, 32)
        go(out_u.at[at], out_u.at[at], peer(dz=2 * d), 14, r_ubz, 64)
    rq2 = rq + zl * 128
    landed(q2, r_qz)
    out_q[rows(rq2, 128), mine] = fold(gq, rq2, 128, q2, 1)
    r_qbz = slot()
    at = rows(rq2, 128)
    go(out_q.at[at, mine], out_q.at[at, mine], peer(dz=1 - 2 * zl), 15, r_qbz, 128)
    three(0)
    three(1)
    two(2)
    two(3)
    landed(out_q.at[rows(rq + (1 - zl) * 128, 128), mine], r_qbz)
    r_qby, r_qc = slot(), slot()
    at = rows(rq, 256)
    for d in (2, 1, 3):
        go(out_q.at[at, mine], out_q.at[at, mine], peer(dy=d), 15, r_qby, 256)
    go(out_q.at[at, mine], out_q.at[at, mine], peer(dc=1), 15, r_qc, 256)
    landed(out_u.at[0:96], r_ubz)
    r_ubx = slot()
    for d in (2, 1, 3):
        at = rows(ru, 128)
        go(out_u.at[at], out_u.at[at], peer(dx=d), 14, r_ubx, 256)
    back_z(0)
    back_z(1)
    three(2)
    three(3)
    back_second(0)
    back_second(1)
    back_z(2)
    back_z(3)
    back_first(0)
    back_first(1)
    back_pair(0, 0)
    back_pair(1, 0)
    back_second(2)
    back_second(3)
    landed(out_q.at[0:768, mine], r_qby)
    for d in (1, 3, 2):
        at = rows(place("y", -d) * 256, 256)
        go(out_q.at[at, mine], out_q.at[at, mine], peer(dc=1), 15, r_qc, 256)
    back_first(2)
    back_first(3)
    back_pair(2, 0)
    back_pair(3, 0)
    for n in (0, 2):
        for d in (1, 3, 2):
            back_pair(n, d)
            back_pair(n + 1, d)
    landed(out_u.at[0:384], r_ubx)
    landed(out_q.at[:, others], r_qc)
    landed(out_r.at[:, others], r_pair)
    left(stat_in, 0)
    left(idx, 1)
    for s in sorted(sent):
        if s > 1:
            left(gr.at[0 : sent[s]], s)


SENDS = 16
RECVS = 56


def per_device(user_states, quot_rows, rem_table, neg_rem, pos_quot, pos_rem):
    vmem = pl.BlockSpec(memory_space=pltpu.VMEM)
    hbm = pl.BlockSpec(memory_space=pltpu.HBM)
    return pl.pallas_call(
        kernel,
        out_shape=(
            pltpu.VMEM((NU, D), F32),
            pltpu.VMEM((NN, D), F32),
            pltpu.VMEM((NR, D), F32),
        ),
        in_specs=[hbm] * 6,
        out_specs=(vmem, vmem, vmem),
        scratch_shapes=[
            pltpu.VMEM((NU, D), BF16),
            pltpu.VMEM((NN, D), BF16),
            pltpu.VMEM((NR, D), BF16),
            pltpu.VMEM((1, NN), jnp.int32),
            pltpu.VMEM((1, NU), jnp.int32),
            pltpu.VMEM((1, NU), jnp.int32),
            pltpu.VMEM((NN, D), F32),
            pltpu.VMEM((NN, D), BF16),
            pltpu.VMEM((NU, D), F32),
            pltpu.VMEM((NU, D), F32),
            pltpu.VMEM((NU, D), F32),
            pltpu.VMEM((NN, NU), F32),
            pltpu.VMEM((NN, NU), BF16),
            pltpu.VMEM((12, 128), F32),
            pltpu.VMEM((15, 12, 128), F32),
            pltpu.VMEM((2, NU), F32),
            pltpu.VMEM((2, NU), F32),
            pltpu.VMEM((2, NN + 2 * NU, H), F32),
            pltpu.VMEM((NN + 2 * NU, H), F32),
            pltpu.VMEM((NN + 2 * NU, D), BF16),
            pltpu.VMEM((2 * NU, D), BF16),
            pltpu.VMEM((NR, H), F32),
            pltpu.VMEM((NN, H), F32),
            pltpu.VMEM((NU, D), F32),
            pltpu.VMEM((4, 3, 256, H), F32),
            pltpu.VMEM((4, 3, 64, H), F32),
            pltpu.VMEM((4, 7, 8, H), F32),
            pltpu.VMEM((3, 256, H), F32),
            pltpu.VMEM((1, 128, H), F32),
            pltpu.VMEM((3, 128, D), F32),
            pltpu.VMEM((3, 32, D), F32),
            pltpu.SemaphoreType.DMA((6,)),
            pltpu.SemaphoreType.DMA((SENDS,)),
            pltpu.SemaphoreType.DMA((RECVS,)),
        ],
        compiler_params=pltpu.CompilerParams(
            collective_id=0, has_side_effects=True, vmem_limit_bytes=58 << 20
        ),
        cost_estimate=pl.CostEstimate(flops=12 << 30, bytes_accessed=9 << 20, transcendentals=1 << 20),
        name="sampled_softmax_grads",
    )(
        user_states, quot_rows, rem_table,
        neg_rem.reshape(1, NN), pos_quot.reshape(1, NU), pos_rem.reshape(1, NU),
    )


def solution(mesh):
    in_specs = (P("user", None), P("item", None), P(), P("item"), P("user"), P("user"))
    out_specs = (P("user", None), P("item", None), P())
    return jax.shard_map(
        per_device, mesh=mesh, in_specs=in_specs, out_specs=out_specs, check_vma=False
    )
```

```python
import functools

import jax
import jax.numpy as jnp
from jax import lax
from jax.experimental import pallas as pl
from jax.experimental.pallas import tpu as pltpu
from jax.sharding import PartitionSpec as P

F32 = jnp.float32
BF16 = jnp.bfloat16
MESH = pl.DeviceIdType.MESH
D = 256
H = 128
NU = 512
NN = 1024
NR = 4096
SCALE = D ** (-0.5)


def coords():
    u = lax.axis_index("user")
    t = lax.axis_index("item")
    return t % 4, u // 4, (t // 4) * 2 + (u // 2) % 2, u % 2


def device(x, y, z, c):
    return (y * 4 + (z % 2) * 2 + c, (z // 2) * 4 + x)


def split_pair(v):
    hi = v.astype(BF16)
    lo = (v - hi.astype(F32)).astype(BF16)
    return hi, lo


def columns_of(row):
    return jnp.transpose(jnp.broadcast_to(row, (128, 128)))


def kernel(
    user_hbm, quot_hbm, rem_hbm, neg_rem_hbm, pos_quot_hbm, pos_rem_hbm,
    out_u, out_q, out_r,
    user, quot, rem, neg_rem, pos_quot, pos_rem,
    remneg, emb, posq, posq_in, pemb, st, pt, stat, stat_in, idx, idx_in, scales, scales_in,
    half, half_in, rhs, rhsq, gr, gq, gu, mid, first_in, second_in, third_in, q1, q2, u1, u2,
    load, send, recv,
):
    x, y, z, c = coords()
    zh, zl = z // 2, z % 2
    t = zh * 4 + x
    mine = pl.ds(pl.multiple_of(c * H, H), H)
    others = pl.ds(pl.multiple_of((1 - c) * H, H), H)

    def peer(dx=0, dy=0, dz=0, dc=0):
        return device((x + dx) % 4, (y + dy) % 4, (z + dz) % 8, (c + dc) % 2)

    item_peers = [(dx, 0, dz, 0) for dz in (0, 2, 4, 6) for dx in range(4) if (dx, dz) != (0, 0)]
    z_peers = [(0, 0, dz, 0) for dz in (1, 3, 5, 7)]
    y_peers = [(0, dy, 0, 0) for dy in (1, 2, 3)]
    peers = item_peers + z_peers + y_peers + [(0, 0, 0, 1)]
    barrier = pltpu.get_barrier_semaphore()
    for p in peers:
        pl.semaphore_signal(barrier, inc=1, device_id=peer(*p), device_id_type=MESH)

    loads = []
    for n, (src, dst) in enumerate((
        (neg_rem_hbm, neg_rem), (rem_hbm, rem), (quot_hbm, quot),
        (pos_rem_hbm, pos_rem), (pos_quot_hbm, pos_quot), (user_hbm, user),
    )):
        loads.append(pltpu.make_async_copy(src, dst, load.at[n]))
        loads[-1].start()

    sent = {}
    recvs = [0]

    def slot():
        recvs[0] += 1
        return recvs[0] - 1

    def go(src, dst, to, s, r, size):
        pltpu.make_async_remote_copy(
            src_ref=src, dst_ref=dst, send_sem=send.at[s], recv_sem=recv.at[r],
            device_id=to, device_id_type=MESH,
        ).start()
        sent[s] = sent.get(s, 0) + size

    def landed(ref, r):
        pltpu.make_async_remote_copy(
            src_ref=ref, dst_ref=ref, send_sem=send.at[0], recv_sem=recv.at[r],
            device_id=peer(dc=1), device_id_type=MESH,
        ).wait_recv()

    def left(ref, s):
        pltpu.make_async_remote_copy(
            src_ref=ref, dst_ref=ref, send_sem=send.at[s], recv_sem=recv.at[0],
            device_id=peer(dc=1), device_id_type=MESH,
        ).wait_send()

    def rows(first_row, count):
        return pl.ds(pl.multiple_of(first_row, 8), count)

    lanes_r = lax.broadcasted_iota(jnp.int32, (256, NR), 1).astype(F32)
    lanes_q = lax.broadcasted_iota(jnp.int32, (256, NN), 1).astype(F32)

    def picks(row_ref, first, shift, lanes):
        parts = []
        for k in range(2):
            at = pl.ds(pl.multiple_of(first + k * 128, 128), 128)
            parts.append(columns_of((row_ref[0:1, at] - shift).astype(F32)))
        col = jnp.concatenate(parts, axis=0)
        wide = jnp.concatenate([col] * (lanes.shape[1] // 128), axis=1)
        return jnp.where(wide == lanes, 1.0, 0.0).astype(BF16)

    def gather_neg(b, carry):
        r0 = pl.multiple_of(b * 256, 256)
        got = jnp.dot(picks(neg_rem, r0, 0, lanes_r), rem[...], preferred_element_type=F32)
        remneg[pl.ds(r0, 256), :] = got
        emb[pl.ds(r0, 256), :] = (quot[pl.ds(r0, 256), :].astype(F32) * got).astype(BF16)
        return carry

    for n in (0, 1, 2):
        loads[n].wait()
    lax.fori_loop(0, NN // 256, gather_neg, 0)
    first = t * NN

    def gather_pos(b, carry):
        r0 = pl.multiple_of(b * 256, 256)
        got_r = jnp.dot(picks(pos_rem, r0, 0, lanes_r), rem[...], preferred_element_type=F32)
        got_q = jnp.dot(picks(pos_quot, r0, first, lanes_q), quot[...], preferred_element_type=F32)
        pemb[pl.ds(r0, 256), :] = (got_q * got_r).astype(BF16).astype(F32)
        own = []
        for k in range(2):
            at = pl.ds(pl.multiple_of(r0 + k * 128, 128), 128)
            col = columns_of((pos_quot[0:1, at] - first).astype(F32))
            own.append((col >= 0.0) & (col < float(NN)))
        own = jnp.concatenate(own, axis=0)
        for h in range(2):
            cols = slice(h * H, (h + 1) * H)
            mask = jnp.where(own, user[pl.ds(r0, 256), cols].astype(F32), 0.0)
            posq[h, 0, pl.ds(r0, 256), :] = mask * got_q[:, cols]
            posq[h, 1, pl.ds(r0, 256), :] = mask * got_r[:, cols]
        return carry

    for n in (3, 4, 5):
        loads[n].wait()
    lax.fori_loop(0, NU // 256, gather_pos, 0)
    idx[0:1, :] = pos_rem[...].astype(F32)
    idx[1:2, :] = (pos_quot[...] - first).astype(F32)

    pl.semaphore_wait(barrier, len(peers))
    r_stat, r_idx, r_half, r_pos, r_coef, r_ux = (slot() for _ in range(6))
    go(idx, idx_in, peer(dc=1), 1, r_idx, 8)
    go(posq.at[1 - c], posq_in, peer(dc=1), 2, r_pos, 2 * NU)

    def scores(b, top):
        r0 = pl.multiple_of(b * 256, 256)
        s = SCALE * lax.dot_general(
            emb[pl.ds(r0, 256), :], user[...], (((1,), (1,)), ((), ())), preferred_element_type=F32
        )
        st[pl.ds(r0, 256), :] = s
        return jnp.maximum(top, jnp.max(s.reshape(32, 8, NU), axis=0))

    top8 = lax.fori_loop(0, NN // 256, scores, jnp.full((8, NU), -jnp.inf, F32))
    top_row = jnp.max(top8, axis=0, keepdims=True)

    def totals(b, tot):
        r0 = pl.multiple_of(b * 256, 256)
        e = jnp.exp(st[pl.ds(r0, 256), :] - top_row)
        pt[pl.ds(r0, 256), :] = e.astype(BF16)
        return tot + jnp.sum(e.reshape(32, 8, NU), axis=0)

    tot8 = lax.fori_loop(0, NN // 256, totals, jnp.zeros((8, NU), F32))
    tot_row = jnp.sum(tot8, axis=0, keepdims=True)
    for k in range(4):
        at = slice(k * 128, (k + 1) * 128)
        stat[k : k + 1, :] = top_row[:, at]
        stat[4 + k : 5 + k, :] = tot_row[:, at]
        prod = user[at, :].astype(F32) * pemb[at, :]
        prod = prod[:, :H] + prod[:, H:]
        stat[8 + k : 9 + k, :] = SCALE * jnp.sum(jnp.transpose(prod), axis=0, keepdims=True)

    for n, p in enumerate(item_peers):
        go(stat, stat_in.at[n], peer(*p), 0, r_stat, 12)

    def users(b, carry):
        at = pl.ds(pl.multiple_of(b * 256, 256), 256)
        g = lax.dot_general(
            pt[at, :], emb[at, :], (((0,), (0,)), ((), ())), preferred_element_type=F32
        )
        gu[...] += g
        return carry

    gu[...] = jnp.zeros_like(gu)
    lax.fori_loop(0, NN // 256, users, 0)
    for d in (1, 3, 2):
        at = rows(((x + d) % 4) * 128, 128)
        go(gu.at[at], u1.at[d - 1], peer(dx=d), 3, r_ux, 256)
        go(pemb.at[at], u1.at[2 + d], peer(dx=d), 3, r_ux, 256)

    landed(stat_in, r_stat)
    tops = [stat[0:4, :]] + [stat_in[n, 0:4, :] for n in range(15)]
    top_neg = functools.reduce(jnp.maximum, tops)
    total = stat[4:8, :] * jnp.exp(tops[0] - top_neg)
    pos_score = stat[8:12, :]
    for n in range(15):
        total = total + stat_in[n, 4:8, :] * jnp.exp(tops[n + 1] - top_neg)
        pos_score = pos_score + stat_in[n, 8:12, :]
    top = jnp.maximum(top_neg, pos_score)
    lse = top + jnp.log(total * jnp.exp(top_neg - top) + jnp.exp(pos_score - top))
    coef = SCALE * (jnp.exp(pos_score - lse) - 1.0)
    scales[0:4, :] = lse
    scales[4:8, :] = coef
    lse_row = jnp.concatenate([lse[k : k + 1, :] for k in range(4)], axis=1)

    go(scales, scales_in, peer(dc=1), 1, r_coef, 8)

    def backward(b, carry):
        r0 = pl.multiple_of(b * 256, 256)
        at = pl.ds(r0, 256)
        p = jnp.exp(st[at, :] - lse_row).astype(BF16)
        g = SCALE * jnp.dot(p, user[...], preferred_element_type=F32)
        half[0, at, :] = g[:, :H]
        half[1, at, :] = g[:, H:]
        return carry

    for k in range(2):
        lax.fori_loop(2 * k, 2 * k + 2, backward, 0)
        at = pl.ds(k * 512, 512)
        go(half.at[1 - c, at], half_in.at[at], peer(dc=1), 2, r_half, 512)

    landed(idx_in, r_idx)
    landed(posq_in, r_pos)

    def scaled(base, src, coefs):
        for k in range(4):
            col = columns_of(coefs[k : k + 1, :])
            at = slice(k * 128, (k + 1) * 128)
            to = slice(base + k * 128, base + (k + 1) * 128)
            hi, lo = split_pair(col * src[0, at, :])
            rhs[NN + to.start : NN + to.stop, :H] = hi
            rhs[NN + to.start : NN + to.stop, H:] = lo
            hi, lo = split_pair(col * src[1, at, :])
            rhsq[to, :H] = hi
            rhsq[to, H:] = lo

    scaled(0, posq.at[c], coef)
    landed(scales_in, r_coef)
    scaled(NU, posq_in, scales_in[4:8, :])

    slots = jnp.concatenate([idx[1:2, :], idx_in[1:2, :]], axis=1)
    down_q = lax.broadcasted_iota(jnp.int32, (256, 2 * NU), 0).astype(F32)
    for b in range(NN // 256):
        pick = jnp.where(down_q + float(b * 256) == slots, 1.0, 0.0).astype(BF16)
        g = jnp.dot(pick, rhsq[...], preferred_element_type=F32)
        gq[b * 256 : (b + 1) * 256, :] = g[:, :H] + g[:, H:]

    landed(half_in, r_half)
    first_half = c == 0

    def pair(first_row):
        def step(b, carry):
            at = rows(first_row + b * 256, 256)
            g = half[c, at, :] + half_in[at, :]
            q = jnp.where(first_half, quot[at, :H].astype(F32), quot[at, H:].astype(F32))
            hi, lo = split_pair(g * q)
            rhs[at, :H] = hi
            rhs[at, H:] = lo
            rn = jnp.where(first_half, remneg[at, :H], remneg[at, H:])
            gq[at, :] += g * rn
            return carry

        lax.fori_loop(0, 2, step, 0)

    r_qz = slot()
    pair((1 - zl) * 512)
    go(gq.at[rows((1 - zl) * 512, 512)], q1.at[0], peer(dz=1 - 2 * zl), 4, r_qz, 512)
    rq = zl * 512
    pair(rq)

    which = jnp.concatenate([neg_rem[...].astype(F32), idx[0:1, :], idx_in[0:1, :]], axis=1)
    down_r = lax.broadcasted_iota(jnp.int32, (256, NN + 2 * NU), 0).astype(F32)
    axes = {"x": x, "y": y}
    order = (2, 1, 3, 0)
    parts = [(0, "x", "y"), (1, "y", "x"), (2, "x", "y"), (3, "y", "x")]
    r_part = [{k: slot() for k in ("one", "two", "three", "z", "s1", "s2", "s3", "f1", "f2", "f3")} for _ in parts]
    r_pair = slot()

    def towards(axis, d):
        return peer(**{"d" + axis: d})

    def place(axis, d=0):
        return (axes[axis] + d) % 4

    def one(n, d):
        p, fst, snd = parts[n]
        r0 = p * 1024 + place(fst, d) * 256
        pick = jnp.where(down_r == which - lax.convert_element_type(r0, F32), 1.0, 0.0).astype(BF16)
        g = jnp.dot(pick, rhs[...], preferred_element_type=F32)
        gr[rows(r0, 256), :] = g[:, :H] + g[:, H:]
        if d:
            go(gr.at[rows(r0, 256)], first_in.at[n, d - 1], towards(fst, d), 5 + n, r_part[n]["one"], 256)

    def fold(dst, r0, count, slots_ref, n):
        v = dst[rows(r0, count), :]
        for k in range(n):
            v = v + slots_ref[k]
        return v

    def base1(n):
        p, fst, snd = parts[n]
        return p * 1024 + place(fst) * 256

    def base2(n):
        return base1(n) + place(parts[n][2]) * 64

    def base3(n):
        return base2(n) + z * 8

    def two(n):
        p, fst, snd = parts[n]
        landed(first_in.at[n], r_part[n]["one"])
        gr[rows(base1(n), 256), :] = fold(gr, base1(n), 256, first_in.at[n], 3)
        for d in (2, 1, 3):
            at = rows(base1(n) + place(snd, d) * 64, 64)
            go(gr.at[at], second_in.at[n, d - 1], towards(snd, d), 5 + n, r_part[n]["two"], 64)

    z_order = (4, 3, 5, 2, 6, 1, 7)

    def three(n):
        landed(second_in.at[n], r_part[n]["two"])
        gr[rows(base2(n), 64), :] = fold(gr, base2(n), 64, second_in.at[n], 3)
        for d in z_order:
            at = rows(base2(n) + ((z + d) % 8) * 8, 8)
            go(gr.at[at], third_in.at[n, d - 1], peer(dz=d), 5 + n, r_part[n]["three"], 8)

    def share(at, to, n, key, size):
        go(out_r.at[at, mine], out_r.at[at, mine], to, 9 + n, r_part[n][key], size)

    def back_z(n):
        landed(third_in.at[n], r_part[n]["three"])
        at = rows(base3(n), 8)
        out_r[at, mine] = fold(gr, base3(n), 8, third_in.at[n], 7)
        for d in z_order:
            share(at, peer(dz=d), n, "z", 8)

    def first_axis(n, at):
        for d in (2, 1, 3):
            share(at, towards(parts[n][1], d), n, f"f{d}", 64)

    def back_second(n):
        landed(out_r.at[0:56, mine], r_part[n]["z"])
        at = rows(base2(n), 64)
        first_axis(n, at)
        for d in (2, 1, 3):
            share(at, towards(parts[n][2], d), n, f"s{d}", 64)

    def back_first(n):
        for d in (1, 3, 2):
            at = rows(base1(n) + place(parts[n][2], -d) * 64, 64)
            landed(out_r.at[at, mine], r_part[n][f"s{d}"])
            first_axis(n, at)

    def to_pair(at):
        go(out_r.at[at, mine], out_r.at[at, mine], peer(dc=1), 13, r_pair, 256)

    def back_pair(n, d):
        p, fst, snd = parts[n]
        at = rows(p * 1024 + place(fst, -d) * 256, 256)
        if d:
            landed(out_r.at[at, mine], r_part[n][f"f{d}"])
        to_pair(at)

    for d in order:
        one(0, d)
        one(1, d)
    ru = x * 128
    landed(u1, r_ux)
    lse_mine = scales[pl.ds(x, 1), :]
    at = rows(ru, 128)
    total_u = jnp.zeros((128, D), F32)
    pos_u = jnp.zeros((128, D), F32)
    for d in range(4):
        top_d = stat_in[d - 1, pl.ds(x, 1), :] if d else stat[pl.ds(x, 1), :]
        col = columns_of(SCALE * jnp.exp(top_d - lse_mine))
        col = jnp.concatenate([col, col], axis=1)
        total_u = total_u + col * (u1[d - 1] if d else gu[at, :])
        pos_u = pos_u + (u1[2 + d] if d else pemb[at, :])
    col = columns_of(scales[pl.ds(4 + x, 1), :])
    mid[...] = total_u + jnp.concatenate([col, col], axis=1) * pos_u
    r_uz = slot()
    for d in (2, 1, 3):
        go(mid.at[rows(((zh + d) % 4) * 32, 32)], u2.at[d - 1], peer(dz=2 * d), 14, r_uz, 64)
    for d in order:
        one(2, d)
        one(3, d)
    landed(q1, r_qz)
    gq[rows(rq, 512), :] = fold(gq, rq, 512, q1, 1)
    r_qy = slot()
    for d in (2, 1, 3):
        at = rows(rq + place("y", d) * 128, 128)
        go(gq.at[at], q2.at[d - 1], peer(dy=d), 15, r_qy, 128)

    two(0)
    two(1)
    ru2 = ru + zh * 32
    landed(u2, r_uz)
    out_u[rows(ru2, 32), :] = fold(mid, zh * 32, 32, u2, 3)
    r_ubz = slot()
    for d in (2, 1, 3):
        at = rows(ru2, 32)
        go(out_u.at[at], out_u.at[at], peer(dz=2 * d), 14, r_ubz, 64)
    three(0)
    three(1)
    rq2 = rq + y * 128
    landed(q2, r_qy)
    out_q[rows(rq2, 128), mine] = fold(gq, rq2, 128, q2, 3)
    r_qby = slot()
    at = rows(rq2, 128)
    for d in (2, 1, 3):
        go(out_q.at[at, mine], out_q.at[at, mine], peer(dy=d), 15, r_qby, 128)
    two(2)
    two(3)
    back_z(0)
    back_z(1)
    landed(out_u.at[0:96], r_ubz)
    r_ubx = slot()
    for d in (2, 1, 3):
        at = rows(ru, 128)
        go(out_u.at[at], out_u.at[at], peer(dx=d), 14, r_ubx, 256)
    three(2)
    three(3)
    landed(out_q.at[0:384, mine], r_qby)
    r_qbz, r_qc = slot(), slot()
    at = rows(rq, 512)
    go(out_q.at[at, mine], out_q.at[at, mine], peer(dz=1 - 2 * zl), 15, r_qbz, 512)
    go(out_q.at[at, mine], out_q.at[at, mine], peer(dc=1), 15, r_qc, 512)
    back_second(0)
    back_second(1)
    back_z(2)
    back_z(3)
    back_first(0)
    back_first(1)
    back_pair(0, 0)
    back_pair(1, 0)
    back_second(2)
    back_second(3)
    at = rows((1 - zl) * 512, 512)
    landed(out_q.at[at, mine], r_qbz)
    go(out_q.at[at, mine], out_q.at[at, mine], peer(dc=1), 15, r_qc, 512)
    back_first(2)
    back_first(3)
    back_pair(2, 0)
    back_pair(3, 0)
    for n in (0, 2):
        for d in (1, 3, 2):
            back_pair(n, d)
            back_pair(n + 1, d)
    landed(out_u.at[0:384], r_ubx)
    landed(out_q.at[:, others], r_qc)
    landed(out_r.at[:, others], r_pair)
    left(stat_in, 0)
    for s in sorted(sent):
        if s > 0:
            left(gr.at[0 : sent[s]], s)


SENDS = 16
RECVS = 56


def per_device(user_states, quot_rows, rem_table, neg_rem, pos_quot, pos_rem):
    vmem = pl.BlockSpec(memory_space=pltpu.VMEM)
    hbm = pl.BlockSpec(memory_space=pltpu.HBM)
    return pl.pallas_call(
        kernel,
        out_shape=(
            pltpu.VMEM((NU, D), F32),
            pltpu.VMEM((NN, D), F32),
            pltpu.VMEM((NR, D), F32),
        ),
        in_specs=[hbm] * 6,
        out_specs=(vmem, vmem, vmem),
        scratch_shapes=[
            pltpu.VMEM((NU, D), BF16),
            pltpu.VMEM((NN, D), BF16),
            pltpu.VMEM((NR, D), BF16),
            pltpu.VMEM((1, NN), jnp.int32),
            pltpu.VMEM((1, NU), jnp.int32),
            pltpu.VMEM((1, NU), jnp.int32),
            pltpu.VMEM((NN, D), F32),
            pltpu.VMEM((NN, D), BF16),
            pltpu.VMEM((2, 2, NU, H), F32),
            pltpu.VMEM((2, NU, H), F32),
            pltpu.VMEM((NU, D), F32),
            pltpu.VMEM((NN, NU), F32),
            pltpu.VMEM((NN, NU), BF16),
            pltpu.VMEM((12, 128), F32),
            pltpu.VMEM((15, 12, 128), F32),
            pltpu.VMEM((2, NU), F32),
            pltpu.VMEM((2, NU), F32),
            pltpu.VMEM((8, 128), F32),
            pltpu.VMEM((8, 128), F32),
            pltpu.VMEM((2, NN, H), F32),
            pltpu.VMEM((NN, H), F32),
            pltpu.VMEM((NN + 2 * NU, D), BF16),
            pltpu.VMEM((2 * NU, D), BF16),
            pltpu.VMEM((NR, H), F32),
            pltpu.VMEM((NN, H), F32),
            pltpu.VMEM((NU, D), F32),
            pltpu.VMEM((128, D), F32),
            pltpu.VMEM((4, 3, 256, H), F32),
            pltpu.VMEM((4, 3, 64, H), F32),
            pltpu.VMEM((4, 7, 8, H), F32),
            pltpu.VMEM((1, 512, H), F32),
            pltpu.VMEM((3, 128, H), F32),
            pltpu.VMEM((6, 128, D), F32),
            pltpu.VMEM((3, 32, D), F32),
            pltpu.SemaphoreType.DMA((6,)),
            pltpu.SemaphoreType.DMA((SENDS,)),
            pltpu.SemaphoreType.DMA((RECVS,)),
        ],
        compiler_params=pltpu.CompilerParams(
            collective_id=0, has_side_effects=True, vmem_limit_bytes=58 << 20
        ),
        cost_estimate=pl.CostEstimate(flops=12 << 30, bytes_accessed=9 << 20, transcendentals=1 << 20),
        name="sampled_softmax_grads",
    )(
        user_states, quot_rows, rem_table,
        neg_rem.reshape(1, NN), pos_quot.reshape(1, NU), pos_rem.reshape(1, NU),
    )


def solution(mesh):
    in_specs = (P("user", None), P("item", None), P(), P("item"), P("user"), P("user"))
    out_specs = (P("user", None), P("item", None), P())
    return jax.shard_map(
        per_device, mesh=mesh, in_specs=in_specs, out_specs=out_specs, check_vma=False
    )
```

```python
import functools

import jax
import jax.numpy as jnp
from jax import lax
from jax.experimental import pallas as pl
from jax.experimental.pallas import tpu as pltpu
from jax.sharding import PartitionSpec as P

F32 = jnp.float32
BF16 = jnp.bfloat16
MESH = pl.DeviceIdType.MESH
D = 256
H = 128
NU = 512
NN = 1024
NR = 4096
SCALE = D ** (-0.5)


def coords():
    u = lax.axis_index("user")
    t = lax.axis_index("item")
    return t % 4, u // 4, (t // 4) * 2 + (u // 2) % 2, u % 2


def device(x, y, z, c):
    return (y * 4 + (z % 2) * 2 + c, (z // 2) * 4 + x)


def split_pair(v):
    hi = v.astype(BF16)
    lo = (v - hi.astype(F32)).astype(BF16)
    return hi, lo


def columns_of(row):
    return jnp.transpose(jnp.broadcast_to(row, (128, 128)))


def kernel(
    user_hbm, quot_hbm, rem_hbm, neg_rem_hbm, pos_quot_hbm, pos_rem_hbm,
    out_u, out_q, out_r,
    user, quot, rem, neg_rem, pos_quot, pos_rem,
    remneg, emb, posq, posq_in, pemb, st, pt, stat, stat_in, idx, idx_in, scales, scales_in,
    half, half_in, low_hot, rhs, rhsq, gr, gq, gu, mid, first_in, second_in, third_in, q1, q2, u1, u2,
    load, send, recv,
):
    x, y, z, c = coords()
    zh, zl = z // 2, z % 2
    t = zh * 4 + x
    mine = pl.ds(pl.multiple_of(c * H, H), H)
    others = pl.ds(pl.multiple_of((1 - c) * H, H), H)

    def peer(dx=0, dy=0, dz=0, dc=0):
        return device((x + dx) % 4, (y + dy) % 4, (z + dz) % 8, (c + dc) % 2)

    item_peers = [(dx, 0, dz, 0) for dz in (0, 2, 4, 6) for dx in range(4) if (dx, dz) != (0, 0)]
    z_peers = [(0, 0, dz, 0) for dz in (1, 3, 5, 7)]
    y_peers = [(0, dy, 0, 0) for dy in (1, 2, 3)]
    peers = item_peers + z_peers + y_peers + [(0, 0, 0, 1)]
    barrier = pltpu.get_barrier_semaphore()
    for p in peers:
        pl.semaphore_signal(barrier, inc=1, device_id=peer(*p), device_id_type=MESH)

    loads = []
    for n, (src, dst) in enumerate((
        (neg_rem_hbm, neg_rem), (rem_hbm, rem), (quot_hbm, quot),
        (pos_rem_hbm, pos_rem), (pos_quot_hbm, pos_quot), (user_hbm, user),
    )):
        loads.append(pltpu.make_async_copy(src, dst, load.at[n]))
        loads[-1].start()

    sent = {}
    recvs = [0]

    def slot():
        recvs[0] += 1
        return recvs[0] - 1

    def go(src, dst, to, s, r, size):
        pltpu.make_async_remote_copy(
            src_ref=src, dst_ref=dst, send_sem=send.at[s], recv_sem=recv.at[r],
            device_id=to, device_id_type=MESH,
        ).start()
        sent[s] = sent.get(s, 0) + size

    def landed(ref, r):
        pltpu.make_async_remote_copy(
            src_ref=ref, dst_ref=ref, send_sem=send.at[0], recv_sem=recv.at[r],
            device_id=peer(dc=1), device_id_type=MESH,
        ).wait_recv()

    def left(ref, s):
        pltpu.make_async_remote_copy(
            src_ref=ref, dst_ref=ref, send_sem=send.at[s], recv_sem=recv.at[0],
            device_id=peer(dc=1), device_id_type=MESH,
        ).wait_send()

    def rows(first_row, count):
        return pl.ds(pl.multiple_of(first_row, 8), count)

    lane = lax.broadcasted_iota(jnp.int32, (128, 128), 1)

    def picks(row_ref, first, shift, width):
        lows, highs = [], []
        for k in range(2):
            at = pl.ds(pl.multiple_of(first + k * 128, 128), 128)
            value = row_ref[0:1, at] - shift
            low = columns_of((value & 127).astype(F32))
            lows.append(jnp.where(low == lane.astype(F32), 1.0, 0.0).astype(BF16))
            highs.append(columns_of((value >> 7).astype(F32)).astype(BF16))
        low, high = jnp.concatenate(lows, axis=0), jnp.concatenate(highs, axis=0)
        zero = jnp.zeros_like(low)
        return jnp.concatenate(
            [jnp.where(high == jnp.full_like(high, k), low, zero) for k in range(width // 128)], axis=1
        )

    def gather_neg(b, carry):
        r0 = pl.multiple_of(b * 256, 256)
        got = jnp.dot(picks(neg_rem, r0, 0, NR), rem[...], preferred_element_type=F32)
        remneg[pl.ds(r0, 256), :] = got
        emb[pl.ds(r0, 256), :] = (quot[pl.ds(r0, 256), :].astype(F32) * got).astype(BF16)
        return carry

    for n in (0, 1, 2):
        loads[n].wait()
    lax.fori_loop(0, NN // 256, gather_neg, 0)
    first = t * NN

    def gather_pos(b, carry):
        r0 = pl.multiple_of(b * 256, 256)
        got_r = jnp.dot(picks(pos_rem, r0, 0, NR), rem[...], preferred_element_type=F32)
        got_q = jnp.dot(picks(pos_quot, r0, first, NN), quot[...], preferred_element_type=F32)
        pemb[pl.ds(r0, 256), :] = (got_q * got_r).astype(BF16).astype(F32)
        own = []
        for k in range(2):
            at = pl.ds(pl.multiple_of(r0 + k * 128, 128), 128)
            col = columns_of((pos_quot[0:1, at] - first).astype(F32))
            own.append((col >= 0.0) & (col < float(NN)))
        own = jnp.concatenate(own, axis=0)
        for h in range(2):
            cols = slice(h * H, (h + 1) * H)
            mask = jnp.where(own, user[pl.ds(r0, 256), cols].astype(F32), 0.0)
            posq[h, 0, pl.ds(r0, 256), :] = mask * got_q[:, cols]
            posq[h, 1, pl.ds(r0, 256), :] = mask * got_r[:, cols]
        return carry

    for n in (3, 4, 5):
        loads[n].wait()
    lax.fori_loop(0, NU // 256, gather_pos, 0)
    idx[0:1, :] = pos_rem[...].astype(F32)
    idx[1:2, :] = (pos_quot[...] - first).astype(F32)

    pl.semaphore_wait(barrier, len(peers))
    r_stat, r_idx, r_half, r_pos, r_coef, r_ux = (slot() for _ in range(6))
    go(idx, idx_in, peer(dc=1), 1, r_idx, 8)
    go(posq.at[1 - c], posq_in, peer(dc=1), 2, r_pos, 2 * NU)

    def scores(b, top):
        r0 = pl.multiple_of(b * 256, 256)
        s = SCALE * lax.dot_general(
            emb[pl.ds(r0, 256), :], user[...], (((1,), (1,)), ((), ())), preferred_element_type=F32
        )
        st[pl.ds(r0, 256), :] = s
        return jnp.maximum(top, jnp.max(s.reshape(32, 8, NU), axis=0))

    top8 = lax.fori_loop(0, NN // 256, scores, jnp.full((8, NU), -jnp.inf, F32))
    top_row = jnp.max(top8, axis=0, keepdims=True)

    def totals(b, tot):
        r0 = pl.multiple_of(b * 256, 256)
        e = jnp.exp(st[pl.ds(r0, 256), :] - top_row)
        pt[pl.ds(r0, 256), :] = e.astype(BF16)
        return tot + jnp.sum(e.reshape(32, 8, NU), axis=0)

    tot8 = lax.fori_loop(0, NN // 256, totals, jnp.zeros((8, NU), F32))
    tot_row = jnp.sum(tot8, axis=0, keepdims=True)
    for k in range(4):
        at = slice(k * 128, (k + 1) * 128)
        stat[k : k + 1, :] = top_row[:, at]
        stat[4 + k : 5 + k, :] = tot_row[:, at]
        prod = user[at, :].astype(F32) * pemb[at, :]
        prod = prod[:, :H] + prod[:, H:]
        stat[8 + k : 9 + k, :] = SCALE * jnp.sum(jnp.transpose(prod), axis=0, keepdims=True)

    for n, p in enumerate(item_peers):
        go(stat, stat_in.at[n], peer(*p), 0, r_stat, 12)

    def users(b, carry):
        at = pl.ds(pl.multiple_of(b * 256, 256), 256)
        g = lax.dot_general(
            pt[at, :], emb[at, :], (((0,), (0,)), ((), ())), preferred_element_type=F32
        )
        gu[...] += g
        return carry

    gu[...] = jnp.zeros_like(gu)
    lax.fori_loop(0, NN // 256, users, 0)
    for d in (1, 3, 2):
        at = rows(((x + d) % 4) * 128, 128)
        go(gu.at[at], u1.at[d - 1], peer(dx=d), 3, r_ux, 256)
        go(pemb.at[at], u1.at[2 + d], peer(dx=d), 3, r_ux, 256)

    landed(idx_in, r_idx)
    which = jnp.concatenate([neg_rem[...].astype(F32), idx[0:1, :], idx_in[0:1, :]], axis=1)
    high = jnp.floor(which * (1.0 / 256.0))
    low = which - 256.0 * high
    for b in range(2):
        down = lax.broadcasted_iota(jnp.int32, (128, NN + 2 * NU), 0).astype(F32) + float(b * 128)
        low_hot[b * 128 : (b + 1) * 128, :] = jnp.where(down == low, 1.0, 0.0).astype(BF16)

    landed(stat_in, r_stat)
    tops = [stat[0:4, :]] + [stat_in[n, 0:4, :] for n in range(15)]
    top_neg = functools.reduce(jnp.maximum, tops)
    total = stat[4:8, :] * jnp.exp(tops[0] - top_neg)
    pos_score = stat[8:12, :]
    for n in range(15):
        total = total + stat_in[n, 4:8, :] * jnp.exp(tops[n + 1] - top_neg)
        pos_score = pos_score + stat_in[n, 8:12, :]
    top = jnp.maximum(top_neg, pos_score)
    lse = top + jnp.log(total * jnp.exp(top_neg - top) + jnp.exp(pos_score - top))
    coef = SCALE * (jnp.exp(pos_score - lse) - 1.0)
    scales[0:4, :] = lse
    scales[4:8, :] = coef
    lse_row = jnp.concatenate([lse[k : k + 1, :] for k in range(4)], axis=1)

    go(scales, scales_in, peer(dc=1), 1, r_coef, 8)

    def backward(b, carry):
        r0 = pl.multiple_of(b * 256, 256)
        at = pl.ds(r0, 256)
        p = jnp.exp(st[at, :] - lse_row).astype(BF16)
        g = SCALE * jnp.dot(p, user[...], preferred_element_type=F32)
        half[0, at, :] = g[:, :H]
        half[1, at, :] = g[:, H:]
        return carry

    for k in range(2):
        lax.fori_loop(2 * k, 2 * k + 2, backward, 0)
        at = pl.ds(k * 512, 512)
        go(half.at[1 - c, at], half_in.at[at], peer(dc=1), 2, r_half, 512)

    landed(posq_in, r_pos)

    def scaled(base, src, coefs):
        for k in range(4):
            col = columns_of(coefs[k : k + 1, :])
            at = slice(k * 128, (k + 1) * 128)
            to = slice(base + k * 128, base + (k + 1) * 128)
            hi, lo = split_pair(col * src[0, at, :])
            rhs[NN + to.start : NN + to.stop, :H] = hi
            rhs[NN + to.start : NN + to.stop, H:] = lo
            hi, lo = split_pair(col * src[1, at, :])
            rhsq[to, :H] = hi
            rhsq[to, H:] = lo

    scaled(0, posq.at[c], coef)
    landed(scales_in, r_coef)
    scaled(NU, posq_in, scales_in[4:8, :])

    slots = jnp.concatenate([idx[1:2, :], idx_in[1:2, :]], axis=1)
    down_q = lax.broadcasted_iota(jnp.int32, (256, 2 * NU), 0).astype(F32)
    for b in range(NN // 256):
        pick = jnp.where(down_q + float(b * 256) == slots, 1.0, 0.0).astype(BF16)
        g = jnp.dot(pick, rhsq[...], preferred_element_type=F32)
        gq[b * 256 : (b + 1) * 256, :] = g[:, :H] + g[:, H:]

    landed(half_in, r_half)
    first_half = c == 0

    def pair(first_row):
        def step(b, carry):
            at = rows(first_row + b * 256, 256)
            g = half[c, at, :] + half_in[at, :]
            q = jnp.where(first_half, quot[at, :H].astype(F32), quot[at, H:].astype(F32))
            hi, lo = split_pair(g * q)
            rhs[at, :H] = hi
            rhs[at, H:] = lo
            rn = jnp.where(first_half, remneg[at, :H], remneg[at, H:])
            gq[at, :] += g * rn
            return carry

        lax.fori_loop(0, 2, step, 0)

    r_qz = slot()
    pair((1 - zl) * 512)
    go(gq.at[rows((1 - zl) * 512, 512)], q1.at[0], peer(dz=1 - 2 * zl), 4, r_qz, 512)
    rq = zl * 512
    pair(rq)

    axes = {"x": x, "y": y}
    order = (2, 1, 3, 0)
    parts = [(0, "x", "y"), (1, "y", "x"), (2, "x", "y"), (3, "y", "x")]
    r_part = [{k: slot() for k in KINDS} for _ in parts]
    r_pair = slot()

    def towards(axis, d):
        return peer(**{"d" + axis: d})

    def place(axis, d=0):
        return (axes[axis] + d) % 4

    def made(n, d):
        p, fst, snd = parts[n]
        r0 = p * 1024 + place(fst, d) * 256
        mask = jnp.where(high == lax.convert_element_type(r0 // 256, F32), 1.0, 0.0).astype(BF16)
        g = jnp.dot(low_hot[...] * mask, rhs[...], preferred_element_type=F32)
        gr[rows(r0, 256), :] = g[:, :H] + g[:, H:]

    def give(n, d):
        p, fst, snd = parts[n]
        r0 = p * 1024 + place(fst, d) * 256
        up, down = rows(r0, 128), rows(r0 + 128, 128)
        if d == 2:
            go(gr.at[up], first_in.at[n, 2, 0:128], towards(fst, 1), 5 + n, r_part[n]["join"], 128)
            go(gr.at[down], first_in.at[n, 2, 128:256], towards(fst, 3), 5 + n, r_part[n]["join"], 128)
        elif d == 1:
            go(gr.at[down], first_in.at[n, 0, 128:256], towards(fst, 1), 5 + n, r_part[n]["one"], 128)
        else:
            go(gr.at[up], first_in.at[n, 1, 0:128], towards(fst, 3), 5 + n, r_part[n]["one"], 128)

    def join(n):
        p, fst, snd = parts[n]
        landed(first_in.at[n, 2], r_part[n]["join"])
        for d, k, h in ((1, 0, 0), (3, 1, 128)):
            at = rows(p * 1024 + place(fst, d) * 256 + h, 128)
            gr[at, :] += first_in[n, 2, h : h + 128, :]
            go(gr.at[at], first_in.at[n, k, h : h + 128], towards(fst, d), 5 + n, r_part[n]["one"], 128)

    def one(n, d):
        made(n, d)
        if d:
            give(n, d)

    def fold(dst, r0, count, slots_ref, n):
        v = dst[rows(r0, count), :]
        for k in range(n):
            v = v + slots_ref[k]
        return v

    def base1(n):
        p, fst, snd = parts[n]
        return p * 1024 + place(fst) * 256

    def base2(n):
        return base1(n) + place(parts[n][2]) * 64

    def base3(n):
        return base2(n) + z * 8

    def two(n):
        p, fst, snd = parts[n]
        landed(first_in.at[n, 0:2], r_part[n]["one"])
        gr[rows(base1(n), 256), :] = fold(gr, base1(n), 256, first_in.at[n], 2)
        for d in (2, 1, 3):
            at = rows(base1(n) + place(snd, d) * 64, 64)
            go(gr.at[at], second_in.at[n, d - 1], towards(snd, d), 5 + n, r_part[n]["two"], 64)

    z_order = (4, 3, 5, 2, 6, 1, 7)

    def three(n):
        landed(second_in.at[n], r_part[n]["two"])
        gr[rows(base2(n), 64), :] = fold(gr, base2(n), 64, second_in.at[n], 3)
        for d in z_order:
            at = rows(base2(n) + ((z + d) % 8) * 8, 8)
            go(gr.at[at], third_in.at[n, d - 1], peer(dz=d), 5 + n, r_part[n]["three"], 8)

    def share(at, to, n, key, size):
        go(out_r.at[at, mine], out_r.at[at, mine], to, 9 + n, r_part[n][key], size)

    def back_z(n):
        landed(third_in.at[n], r_part[n]["three"])
        at = rows(base3(n), 8)
        out_r[at, mine] = fold(gr, base3(n), 8, third_in.at[n], 7)
        for d in z_order:
            share(at, peer(dz=d), n, "z", 8)

    def first_axis(n, k):
        at = rows(base1(n) + place(parts[n][2], -k) * 64, 64)
        for d in (1, 3):
            share(at, towards(parts[n][1], d), n, f"f{d}_{k}", 64)

    def pass_on(n, k):
        p, fst, snd = parts[n]
        for d, h in ((1, 0), (3, 32)):
            r0 = p * 1024 + place(fst, -d) * 256 + place(snd, -k) * 64
            landed(out_r.at[rows(r0, 64), mine], r_part[n][f"f{d}_{k}"])
            share(rows(r0 + h, 32), towards(fst, d), n, f"h{d}", 32)

    def back_second(n):
        landed(out_r.at[0:56, mine], r_part[n]["z"])
        at = rows(base2(n), 64)
        first_axis(n, 0)
        for d in (2, 1, 3):
            share(at, towards(parts[n][2], d), n, f"s{d}", 64)

    def back_first(n):
        for d in (1, 3, 2):
            at = rows(base1(n) + place(parts[n][2], -d) * 64, 64)
            landed(out_r.at[at, mine], r_part[n][f"s{d}"])
            first_axis(n, d)

    def to_pair(at):
        go(out_r.at[at, mine], out_r.at[at, mine], peer(dc=1), 13, r_pair, 256)

    def back_pair(n, d):
        p, fst, snd = parts[n]
        at = rows(p * 1024 + place(fst, -d) * 256, 256)
        if d == 2:
            landed(out_r.at[0:128, mine], r_part[n]["h1"])
            landed(out_r.at[0:128, mine], r_part[n]["h3"])
        to_pair(at)

    for d in order:
        one(0, d)
        one(1, d)
    join(0)
    join(1)
    ru = x * 128
    landed(u1, r_ux)
    lse_mine = scales[pl.ds(x, 1), :]
    at = rows(ru, 128)
    total_u = jnp.zeros((128, D), F32)
    pos_u = jnp.zeros((128, D), F32)
    for d in range(4):
        top_d = stat_in[d - 1, pl.ds(x, 1), :] if d else stat[pl.ds(x, 1), :]
        col = columns_of(SCALE * jnp.exp(top_d - lse_mine))
        col = jnp.concatenate([col, col], axis=1)
        total_u = total_u + col * (u1[d - 1] if d else gu[at, :])
        pos_u = pos_u + (u1[2 + d] if d else pemb[at, :])
    col = columns_of(scales[pl.ds(4 + x, 1), :])
    mid[...] = total_u + jnp.concatenate([col, col], axis=1) * pos_u
    r_uz = slot()
    for d in (2, 1, 3):
        go(mid.at[rows(((zh + d) % 4) * 32, 32)], u2.at[d - 1], peer(dz=2 * d), 14, r_uz, 64)
    for d in order:
        one(2, d)
        one(3, d)
    join(2)
    join(3)
    two(0)
    two(1)
    two(2)
    two(3)
    landed(q1, r_qz)
    gq[rows(rq, 512), :] = fold(gq, rq, 512, q1, 1)
    r_qy = slot()
    for d in (2, 1, 3):
        at = rows(rq + place("y", d) * 128, 128)
        go(gq.at[at], q2.at[d - 1], peer(dy=d), 15, r_qy, 128)
    three(0)
    three(1)
    ru2 = ru + zh * 32
    landed(u2, r_uz)
    out_u[rows(ru2, 32), :] = fold(mid, zh * 32, 32, u2, 3)
    r_ubz = slot()
    for d in (2, 1, 3):
        at = rows(ru2, 32)
        go(out_u.at[at], out_u.at[at], peer(dz=2 * d), 14, r_ubz, 64)
    three(2)
    three(3)
    rq2 = rq + y * 128
    landed(q2, r_qy)
    out_q[rows(rq2, 128), mine] = fold(gq, rq2, 128, q2, 3)
    r_qby = slot()
    at = rows(rq2, 128)
    for d in (2, 1, 3):
        go(out_q.at[at, mine], out_q.at[at, mine], peer(dy=d), 15, r_qby, 128)
    back_z(0)
    back_z(1)
    back_z(2)
    back_z(3)
    landed(out_u.at[0:96], r_ubz)
    r_ub1, r_ub3, r_uh = slot(), slot(), slot()
    at = rows(ru, 128)
    go(out_u.at[at], out_u.at[at], peer(dx=1), 14, r_ub1, 256)
    go(out_u.at[at], out_u.at[at], peer(dx=3), 14, r_ub3, 256)
    landed(out_q.at[0:384, mine], r_qby)
    r_qbz, r_qc = slot(), slot()
    at = rows(rq, 512)
    go(out_q.at[at, mine], out_q.at[at, mine], peer(dz=1 - 2 * zl), 15, r_qbz, 512)
    go(out_q.at[at, mine], out_q.at[at, mine], peer(dc=1), 15, r_qc, 512)
    back_second(0)
    back_second(1)
    back_second(2)
    back_second(3)
    pass_on(0, 0)
    pass_on(1, 0)
    pass_on(2, 0)
    pass_on(3, 0)
    for d, h, r in ((1, 0, r_ub1), (3, 64, r_ub3)):
        r0 = ((x - d) % 4) * 128
        landed(out_u.at[rows(r0, 128)], r)
        at = rows(r0 + h, 64)
        go(out_u.at[at], out_u.at[at], peer(dx=d), 14, r_uh, 128)
    back_first(0)
    back_first(1)
    back_first(2)
    back_first(3)
    back_pair(0, 0)
    back_pair(1, 0)
    back_pair(2, 0)
    back_pair(3, 0)
    for k in (1, 3, 2):
        pass_on(0, k)
        pass_on(1, k)
    for k in (1, 3, 2):
        pass_on(2, k)
        pass_on(3, k)
    at = rows((1 - zl) * 512, 512)
    landed(out_q.at[at, mine], r_qbz)
    go(out_q.at[at, mine], out_q.at[at, mine], peer(dc=1), 15, r_qc, 512)
    for d in (1, 3, 2):
        back_pair(0, d)
        back_pair(1, d)
    for d in (1, 3, 2):
        back_pair(2, d)
        back_pair(3, d)
    landed(out_u.at[0:128], r_uh)
    landed(out_q.at[:, others], r_qc)
    landed(out_r.at[:, others], r_pair)
    left(stat_in, 0)
    for s in sorted(sent):
        if s > 0:
            left(gr.at[0 : sent[s]], s)


KINDS = ("join", "one", "two", "three", "z", "s1", "s2", "s3", "h1", "h3") + tuple(
    f"f{d}_{k}" for d in (1, 3) for k in range(4)
)
SENDS = 16
RECVS = 92


def per_device(user_states, quot_rows, rem_table, neg_rem, pos_quot, pos_rem):
    vmem = pl.BlockSpec(memory_space=pltpu.VMEM)
    hbm = pl.BlockSpec(memory_space=pltpu.HBM)
    return pl.pallas_call(
        kernel,
        out_shape=(
            pltpu.VMEM((NU, D), F32),
            pltpu.VMEM((NN, D), F32),
            pltpu.VMEM((NR, D), F32),
        ),
        in_specs=[hbm] * 6,
        out_specs=(vmem, vmem, vmem),
        scratch_shapes=[
            pltpu.VMEM((NU, D), BF16),
            pltpu.VMEM((NN, D), BF16),
            pltpu.VMEM((NR, D), BF16),
            pltpu.VMEM((1, NN), jnp.int32),
            pltpu.VMEM((1, NU), jnp.int32),
            pltpu.VMEM((1, NU), jnp.int32),
            pltpu.VMEM((NN, D), F32),
            pltpu.VMEM((NN, D), BF16),
            pltpu.VMEM((2, 2, NU, H), F32),
            pltpu.VMEM((2, NU, H), F32),
            pltpu.VMEM((NU, D), F32),
            pltpu.VMEM((NN, NU), F32),
            pltpu.VMEM((NN, NU), BF16),
            pltpu.VMEM((12, 128), F32),
            pltpu.VMEM((15, 12, 128), F32),
            pltpu.VMEM((2, NU), F32),
            pltpu.VMEM((2, NU), F32),
            pltpu.VMEM((8, 128), F32),
            pltpu.VMEM((8, 128), F32),
            pltpu.VMEM((2, NN, H), F32),
            pltpu.VMEM((NN, H), F32),
            pltpu.VMEM((256, NN + 2 * NU), BF16),
            pltpu.VMEM((NN + 2 * NU, D), BF16),
            pltpu.VMEM((2 * NU, D), BF16),
            pltpu.VMEM((NR, H), F32),
            pltpu.VMEM((NN, H), F32),
            pltpu.VMEM((NU, D), F32),
            pltpu.VMEM((128, D), F32),
            pltpu.VMEM((4, 3, 256, H), F32),
            pltpu.VMEM((4, 3, 64, H), F32),
            pltpu.VMEM((4, 7, 8, H), F32),
            pltpu.VMEM((1, 512, H), F32),
            pltpu.VMEM((3, 128, H), F32),
            pltpu.VMEM((6, 128, D), F32),
            pltpu.VMEM((3, 32, D), F32),
            pltpu.SemaphoreType.DMA((6,)),
            pltpu.SemaphoreType.DMA((SENDS,)),
            pltpu.SemaphoreType.DMA((RECVS,)),
        ],
        compiler_params=pltpu.CompilerParams(
            collective_id=0, has_side_effects=True, vmem_limit_bytes=58 << 20
        ),
        cost_estimate=pl.CostEstimate(flops=12 << 30, bytes_accessed=9 << 20, transcendentals=1 << 20),
        name="sampled_softmax_grads",
    )(
        user_states, quot_rows, rem_table,
        neg_rem.reshape(1, NN), pos_quot.reshape(1, NU), pos_rem.reshape(1, NU),
    )


def solution(mesh):
    in_specs = (P("user", None), P("item", None), P(), P("item"), P("user"), P("user"))
    out_specs = (P("user", None), P("item", None), P())
    return jax.shard_map(
        per_device, mesh=mesh, in_specs=in_specs, out_specs=out_specs, check_vma=False
    )
```

```python
import functools

import jax
import jax.numpy as jnp
from jax import lax
from jax.experimental import pallas as pl
from jax.experimental.pallas import tpu as pltpu
from jax.sharding import PartitionSpec as P

F32 = jnp.float32
BF16 = jnp.bfloat16
MESH = pl.DeviceIdType.MESH
D = 256
H = 128
NU = 512
NN = 1024
NR = 4096
SCALE = D ** (-0.5)


def coords():
    u = lax.axis_index("user")
    t = lax.axis_index("item")
    return t % 4, u // 4, (t // 4) * 2 + (u // 2) % 2, u % 2


def device(x, y, z, c):
    return (y * 4 + (z % 2) * 2 + c, (z // 2) * 4 + x)


def split_pair(v):
    hi = v.astype(BF16)
    lo = (v - hi.astype(F32)).astype(BF16)
    return hi, lo


def columns_of(row):
    return jnp.transpose(jnp.broadcast_to(row, (128, 128)))


def kernel(
    user_hbm, quot_hbm, rem_hbm, neg_rem_hbm, pos_quot_hbm, pos_rem_hbm,
    out_u, out_q, out_r,
    user, quot, rem, neg_rem, pos_quot, pos_rem,
    remneg, emb, posq, posq_in, pemb, st, pt, stat, stat_in, idx, idx_in, scales, scales_in,
    half, half_in, low_hot, rhs, rhsq, gr, gq, gu, mid, first_in, second_in, third_in, q1, q2, u1, u2,
    load, send, recv,
):
    x, y, z, c = coords()
    zh, zl = z // 2, z % 2
    t = zh * 4 + x
    mine = pl.ds(pl.multiple_of(c * H, H), H)
    others = pl.ds(pl.multiple_of((1 - c) * H, H), H)

    def peer(dx=0, dy=0, dz=0, dc=0):
        return device((x + dx) % 4, (y + dy) % 4, (z + dz) % 8, (c + dc) % 2)

    item_peers = [(dx, 0, dz, 0) for dz in (0, 2, 4, 6) for dx in range(4) if (dx, dz) != (0, 0)]
    z_peers = [(0, 0, dz, 0) for dz in (1, 3, 5, 7)]
    y_peers = [(0, dy, 0, 0) for dy in (1, 2, 3)]
    peers = item_peers + z_peers + y_peers + [(0, 0, 0, 1)]
    barrier = pltpu.get_barrier_semaphore()
    for p in peers:
        pl.semaphore_signal(barrier, inc=1, device_id=peer(*p), device_id_type=MESH)

    loads = []
    for n, (src, dst) in enumerate((
        (neg_rem_hbm, neg_rem), (rem_hbm, rem), (quot_hbm, quot),
        (pos_rem_hbm, pos_rem), (pos_quot_hbm, pos_quot), (user_hbm, user),
    )):
        loads.append(pltpu.make_async_copy(src, dst, load.at[n]))
        loads[-1].start()

    sent = {}
    recvs = [0]

    def slot():
        recvs[0] += 1
        return recvs[0] - 1

    def go(src, dst, to, s, r, size):
        pltpu.make_async_remote_copy(
            src_ref=src, dst_ref=dst, send_sem=send.at[s], recv_sem=recv.at[r],
            device_id=to, device_id_type=MESH,
        ).start()
        sent[s] = sent.get(s, 0) + size

    def landed(ref, r):
        pltpu.make_async_remote_copy(
            src_ref=ref, dst_ref=ref, send_sem=send.at[0], recv_sem=recv.at[r],
            device_id=peer(dc=1), device_id_type=MESH,
        ).wait_recv()

    def left(ref, s):
        pltpu.make_async_remote_copy(
            src_ref=ref, dst_ref=ref, send_sem=send.at[s], recv_sem=recv.at[0],
            device_id=peer(dc=1), device_id_type=MESH,
        ).wait_send()

    def rows(first_row, count):
        return pl.ds(pl.multiple_of(first_row, 8), count)

    lane = lax.broadcasted_iota(jnp.int32, (128, 128), 1)

    def picks(row_ref, first, shift, width):
        lows, highs = [], []
        for k in range(2):
            at = pl.ds(pl.multiple_of(first + k * 128, 128), 128)
            value = row_ref[0:1, at] - shift
            low = columns_of((value & 127).astype(F32))
            lows.append(jnp.where(low == lane.astype(F32), 1.0, 0.0).astype(BF16))
            highs.append(columns_of((value >> 7).astype(F32)).astype(BF16))
        low, high = jnp.concatenate(lows, axis=0), jnp.concatenate(highs, axis=0)
        zero = jnp.zeros_like(low)
        return jnp.concatenate(
            [jnp.where(high == jnp.full_like(high, k), low, zero) for k in range(width // 128)], axis=1
        )

    def gather_neg(b, carry):
        r0 = pl.multiple_of(b * 256, 256)
        got = jnp.dot(picks(neg_rem, r0, 0, NR), rem[...], preferred_element_type=F32)
        remneg[pl.ds(r0, 256), :] = got
        emb[pl.ds(r0, 256), :] = (quot[pl.ds(r0, 256), :].astype(F32) * got).astype(BF16)
        return carry

    for n in (0, 1, 2):
        loads[n].wait()
    lax.fori_loop(0, NN // 256, gather_neg, 0)
    first = t * NN

    def gather_pos(b, carry):
        r0 = pl.multiple_of(b * 256, 256)
        got_r = jnp.dot(picks(pos_rem, r0, 0, NR), rem[...], preferred_element_type=F32)
        got_q = jnp.dot(picks(pos_quot, r0, first, NN), quot[...], preferred_element_type=F32)
        pemb[pl.ds(r0, 256), :] = (got_q * got_r).astype(BF16).astype(F32)
        own = []
        for k in range(2):
            at = pl.ds(pl.multiple_of(r0 + k * 128, 128), 128)
            col = columns_of((pos_quot[0:1, at] - first).astype(F32))
            own.append((col >= 0.0) & (col < float(NN)))
        own = jnp.concatenate(own, axis=0)
        for h in range(2):
            cols = slice(h * H, (h + 1) * H)
            mask = jnp.where(own, user[pl.ds(r0, 256), cols].astype(F32), 0.0)
            posq[h, 0, pl.ds(r0, 256), :] = mask * got_q[:, cols]
            posq[h, 1, pl.ds(r0, 256), :] = mask * got_r[:, cols]
        return carry

    for n in (3, 4, 5):
        loads[n].wait()
    lax.fori_loop(0, NU // 256, gather_pos, 0)
    idx[0:1, :] = pos_rem[...].astype(F32)
    idx[1:2, :] = (pos_quot[...] - first).astype(F32)

    pl.semaphore_wait(barrier, len(peers))
    r_stat, r_idx, r_half, r_pos, r_coef, r_ux = (slot() for _ in range(6))
    go(idx, idx_in, peer(dc=1), 1, r_idx, 8)
    go(posq.at[1 - c], posq_in, peer(dc=1), 2, r_pos, 2 * NU)

    def scores(b, top):
        r0 = pl.multiple_of(b * 256, 256)
        s = SCALE * lax.dot_general(
            emb[pl.ds(r0, 256), :], user[...], (((1,), (1,)), ((), ())), preferred_element_type=F32
        )
        st[pl.ds(r0, 256), :] = s
        return jnp.maximum(top, jnp.max(s.reshape(32, 8, NU), axis=0))

    top8 = lax.fori_loop(0, NN // 256, scores, jnp.full((8, NU), -jnp.inf, F32))
    top_row = jnp.max(top8, axis=0, keepdims=True)

    def totals(b, tot):
        r0 = pl.multiple_of(b * 256, 256)
        e = jnp.exp(st[pl.ds(r0, 256), :] - top_row)
        pt[pl.ds(r0, 256), :] = e.astype(BF16)
        return tot + jnp.sum(e.reshape(32, 8, NU), axis=0)

    tot8 = lax.fori_loop(0, NN // 256, totals, jnp.zeros((8, NU), F32))
    tot_row = jnp.sum(tot8, axis=0, keepdims=True)
    for k in range(4):
        at = slice(k * 128, (k + 1) * 128)
        stat[k : k + 1, :] = top_row[:, at]
        stat[4 + k : 5 + k, :] = tot_row[:, at]
        prod = user[at, :].astype(F32) * pemb[at, :]
        prod = prod[:, :H] + prod[:, H:]
        stat[8 + k : 9 + k, :] = SCALE * jnp.sum(jnp.transpose(prod), axis=0, keepdims=True)

    for n, p in enumerate(item_peers):
        go(stat, stat_in.at[n], peer(*p), 0, r_stat, 12)

    def users(b, carry):
        at = pl.ds(pl.multiple_of(b * 256, 256), 256)
        g = lax.dot_general(
            pt[at, :], emb[at, :], (((0,), (0,)), ((), ())), preferred_element_type=F32
        )
        gu[...] += g
        return carry

    gu[...] = jnp.zeros_like(gu)
    lax.fori_loop(0, NN // 256, users, 0)
    for d in (1, 3, 2):
        at = rows(((x + d) % 4) * 128, 128)
        go(gu.at[at], u1.at[d - 1], peer(dx=d), 3, r_ux, 256)
        go(pemb.at[at], u1.at[2 + d], peer(dx=d), 3, r_ux, 256)

    landed(idx_in, r_idx)
    which = jnp.concatenate([neg_rem[...].astype(F32), idx[0:1, :], idx_in[0:1, :]], axis=1)
    high = jnp.floor(which * (1.0 / 256.0))
    low = which - 256.0 * high
    for b in range(2):
        down = lax.broadcasted_iota(jnp.int32, (128, NN + 2 * NU), 0).astype(F32) + float(b * 128)
        low_hot[b * 128 : (b + 1) * 128, :] = jnp.where(down == low, 1.0, 0.0).astype(BF16)

    landed(stat_in, r_stat)
    tops = [stat[0:4, :]] + [stat_in[n, 0:4, :] for n in range(15)]
    top_neg = functools.reduce(jnp.maximum, tops)
    total = stat[4:8, :] * jnp.exp(tops[0] - top_neg)
    pos_score = stat[8:12, :]
    for n in range(15):
        total = total + stat_in[n, 4:8, :] * jnp.exp(tops[n + 1] - top_neg)
        pos_score = pos_score + stat_in[n, 8:12, :]
    top = jnp.maximum(top_neg, pos_score)
    lse = top + jnp.log(total * jnp.exp(top_neg - top) + jnp.exp(pos_score - top))
    coef = SCALE * (jnp.exp(pos_score - lse) - 1.0)
    scales[0:4, :] = lse
    scales[4:8, :] = coef
    lse_row = jnp.concatenate([lse[k : k + 1, :] for k in range(4)], axis=1)

    go(scales, scales_in, peer(dc=1), 1, r_coef, 8)

    def backward(b, carry):
        r0 = pl.multiple_of(b * 256, 256)
        at = pl.ds(r0, 256)
        p = jnp.exp(st[at, :] - lse_row).astype(BF16)
        g = SCALE * jnp.dot(p, user[...], preferred_element_type=F32)
        half[0, at, :] = g[:, :H]
        half[1, at, :] = g[:, H:]
        return carry

    for k in range(2):
        lax.fori_loop(2 * k, 2 * k + 2, backward, 0)
        at = pl.ds(k * 512, 512)
        go(half.at[1 - c, at], half_in.at[at], peer(dc=1), 2, r_half, 512)

    landed(posq_in, r_pos)

    def scaled(base, src, coefs):
        for k in range(4):
            col = columns_of(coefs[k : k + 1, :])
            at = slice(k * 128, (k + 1) * 128)
            to = slice(base + k * 128, base + (k + 1) * 128)
            hi, lo = split_pair(col * src[0, at, :])
            rhs[NN + to.start : NN + to.stop, :H] = hi
            rhs[NN + to.start : NN + to.stop, H:] = lo
            hi, lo = split_pair(col * src[1, at, :])
            rhsq[to, :H] = hi
            rhsq[to, H:] = lo

    scaled(0, posq.at[c], coef)
    landed(scales_in, r_coef)
    scaled(NU, posq_in, scales_in[4:8, :])

    slots = jnp.concatenate([idx[1:2, :], idx_in[1:2, :]], axis=1)
    down_q = lax.broadcasted_iota(jnp.int32, (256, 2 * NU), 0).astype(F32)
    for b in range(NN // 256):
        pick = jnp.where(down_q + float(b * 256) == slots, 1.0, 0.0).astype(BF16)
        g = jnp.dot(pick, rhsq[...], preferred_element_type=F32)
        gq[b * 256 : (b + 1) * 256, :] = g[:, :H] + g[:, H:]

    landed(half_in, r_half)
    first_half = c == 0

    def pair(first_row):
        def step(b, carry):
            at = rows(first_row + b * 256, 256)
            g = half[c, at, :] + half_in[at, :]
            q = jnp.where(first_half, quot[at, :H].astype(F32), quot[at, H:].astype(F32))
            hi, lo = split_pair(g * q)
            rhs[at, :H] = hi
            rhs[at, H:] = lo
            rn = jnp.where(first_half, remneg[at, :H], remneg[at, H:])
            gq[at, :] += g * rn
            return carry

        lax.fori_loop(0, 2, step, 0)

    r_qz = slot()
    pair((1 - zl) * 512)
    go(gq.at[rows((1 - zl) * 512, 512)], q1.at[0], peer(dz=1 - 2 * zl), 4, r_qz, 512)
    rq = zl * 512
    pair(rq)

    axes = {"x": x, "y": y}
    order = (2, 1, 3, 0)
    parts = [(0, "x", "y"), (1, "y", "x"), (2, "x", "y"), (3, "y", "x")]
    r_part = [{k: slot() for k in KINDS} for _ in parts]
    r_pair = slot()

    def towards(axis, d):
        return peer(**{"d" + axis: d})

    def place(axis, d=0):
        return (axes[axis] + d) % 4

    def made(n, d):
        p, fst, snd = parts[n]
        r0 = p * 1024 + place(fst, d) * 256
        mask = jnp.where(high == lax.convert_element_type(r0 // 256, F32), 1.0, 0.0).astype(BF16)
        g = jnp.dot(low_hot[...] * mask, rhs[...], preferred_element_type=F32)
        gr[rows(r0, 256), :] = g[:, :H] + g[:, H:]

    def give(n, d):
        p, fst, snd = parts[n]
        r0 = p * 1024 + place(fst, d) * 256
        up, down = rows(r0, 128), rows(r0 + 128, 128)
        if d == 2:
            go(gr.at[up], first_in.at[n, 2, 0:128], towards(fst, 1), 5 + n, r_part[n]["join"], 128)
            go(gr.at[down], first_in.at[n, 2, 128:256], towards(fst, 3), 5 + n, r_part[n]["join"], 128)
        elif d == 1:
            go(gr.at[down], first_in.at[n, 0, 128:256], towards(fst, 1), 5 + n, r_part[n]["one"], 128)
        else:
            go(gr.at[up], first_in.at[n, 1, 0:128], towards(fst, 3), 5 + n, r_part[n]["one"], 128)

    def join(n):
        p, fst, snd = parts[n]
        landed(first_in.at[n, 2], r_part[n]["join"])
        for d, k, h in ((1, 0, 0), (3, 1, 128)):
            at = rows(p * 1024 + place(fst, d) * 256 + h, 128)
            gr[at, :] += first_in[n, 2, h : h + 128, :]
            go(gr.at[at], first_in.at[n, k, h : h + 128], towards(fst, d), 5 + n, r_part[n]["one"], 128)

    def one(n, d):
        made(n, d)
        if d:
            give(n, d)

    def fold(dst, r0, count, slots_ref, n):
        v = dst[rows(r0, count), :]
        for k in range(n):
            v = v + slots_ref[k]
        return v

    def base1(n):
        p, fst, snd = parts[n]
        return p * 1024 + place(fst) * 256

    def base2(n):
        return base1(n) + place(parts[n][2]) * 64

    def base3(n):
        return base2(n) + z * 8

    def two(n):
        p, fst, snd = parts[n]
        landed(first_in.at[n, 0:2], r_part[n]["one"])
        gr[rows(base1(n), 256), :] = fold(gr, base1(n), 256, first_in.at[n], 2)
        for d in (2, 1, 3):
            at = rows(base1(n) + place(snd, d) * 64, 64)
            go(gr.at[at], second_in.at[n, d - 1], towards(snd, d), 5 + n, r_part[n]["two"], 64)

    z_order = (4, 3, 5, 2, 6, 1, 7)

    def three(n):
        landed(second_in.at[n], r_part[n]["two"])
        gr[rows(base2(n), 64), :] = fold(gr, base2(n), 64, second_in.at[n], 3)
        for d in z_order:
            at = rows(base2(n) + ((z + d) % 8) * 8, 8)
            go(gr.at[at], third_in.at[n, d - 1], peer(dz=d), 5 + n, r_part[n]["three"], 8)

    def share(at, to, n, key, size):
        go(out_r.at[at, mine], out_r.at[at, mine], to, 9 + n, r_part[n][key], size)

    def back_z(n):
        landed(third_in.at[n], r_part[n]["three"])
        at = rows(base3(n), 8)
        out_r[at, mine] = fold(gr, base3(n), 8, third_in.at[n], 7)
        for d in z_order:
            share(at, peer(dz=d), n, "z", 8)

    def first_axis(n, k):
        at = rows(base1(n) + place(parts[n][2], -k) * 64, 64)
        for d in (1, 3):
            share(at, towards(parts[n][1], d), n, f"f{d}_{k}", 64)

    def pass_on(n, k):
        p, fst, snd = parts[n]
        for d, h in ((1, 0), (3, 32)):
            r0 = p * 1024 + place(fst, -d) * 256 + place(snd, -k) * 64
            landed(out_r.at[rows(r0, 64), mine], r_part[n][f"f{d}_{k}"])
            share(rows(r0 + h, 32), towards(fst, d), n, f"h{d}", 32)

    def back_second(n):
        landed(out_r.at[0:56, mine], r_part[n]["z"])
        at = rows(base2(n), 64)
        first_axis(n, 0)
        for d in (2, 1, 3):
            share(at, towards(parts[n][2], d), n, f"s{d}", 64)

    def back_first(n):
        for d in (1, 3, 2):
            at = rows(base1(n) + place(parts[n][2], -d) * 64, 64)
            landed(out_r.at[at, mine], r_part[n][f"s{d}"])
            first_axis(n, d)

    def to_pair(at):
        go(out_r.at[at, mine], out_r.at[at, mine], peer(dc=1), 13, r_pair, 256)

    def back_pair(n, d):
        p, fst, snd = parts[n]
        at = rows(p * 1024 + place(fst, -d) * 256, 256)
        if d == 2:
            landed(out_r.at[0:128, mine], r_part[n]["h1"])
            landed(out_r.at[0:128, mine], r_part[n]["h3"])
        to_pair(at)

    for d in order:
        for n in range(4):
            one(n, d)
    join(0)
    join(1)
    join(2)
    join(3)
    ru = x * 128
    landed(u1, r_ux)
    lse_mine = scales[pl.ds(x, 1), :]
    at = rows(ru, 128)
    total_u = jnp.zeros((128, D), F32)
    pos_u = jnp.zeros((128, D), F32)
    for d in range(4):
        top_d = stat_in[d - 1, pl.ds(x, 1), :] if d else stat[pl.ds(x, 1), :]
        col = columns_of(SCALE * jnp.exp(top_d - lse_mine))
        col = jnp.concatenate([col, col], axis=1)
        total_u = total_u + col * (u1[d - 1] if d else gu[at, :])
        pos_u = pos_u + (u1[2 + d] if d else pemb[at, :])
    col = columns_of(scales[pl.ds(4 + x, 1), :])
    mid[...] = total_u + jnp.concatenate([col, col], axis=1) * pos_u
    r_uz = slot()
    for d in (2, 1, 3):
        go(mid.at[rows(((zh + d) % 4) * 32, 32)], u2.at[d - 1], peer(dz=2 * d), 14, r_uz, 64)
    two(0)
    two(1)
    two(2)
    two(3)
    ru2 = ru + zh * 32
    landed(u2, r_uz)
    out_u[rows(ru2, 32), :] = fold(mid, zh * 32, 32, u2, 3)
    r_ubz = slot()
    for d in (2, 1, 3):
        at = rows(ru2, 32)
        go(out_u.at[at], out_u.at[at], peer(dz=2 * d), 14, r_ubz, 64)
    landed(q1, r_qz)
    gq[rows(rq, 512), :] = fold(gq, rq, 512, q1, 1)
    r_qy = slot()
    for d in (2, 1, 3):
        at = rows(rq + place("y", d) * 128, 128)
        go(gq.at[at], q2.at[d - 1], peer(dy=d), 15, r_qy, 128)
    three(0)
    three(1)
    three(2)
    three(3)
    landed(out_u.at[0:96], r_ubz)
    r_ub1, r_ub3, r_uh = slot(), slot(), slot()
    at = rows(ru, 128)
    go(out_u.at[at], out_u.at[at], peer(dx=1), 14, r_ub1, 256)
    go(out_u.at[at], out_u.at[at], peer(dx=3), 14, r_ub3, 256)
    rq2 = rq + y * 128
    landed(q2, r_qy)
    out_q[rows(rq2, 128), mine] = fold(gq, rq2, 128, q2, 3)
    r_qby = slot()
    at = rows(rq2, 128)
    for d in (2, 1, 3):
        go(out_q.at[at, mine], out_q.at[at, mine], peer(dy=d), 15, r_qby, 128)
    back_z(0)
    back_z(1)
    back_z(2)
    back_z(3)
    landed(out_q.at[0:384, mine], r_qby)
    r_qbz, r_qc = slot(), slot()
    at = rows(rq, 512)
    go(out_q.at[at, mine], out_q.at[at, mine], peer(dz=1 - 2 * zl), 15, r_qbz, 512)
    go(out_q.at[at, mine], out_q.at[at, mine], peer(dc=1), 15, r_qc, 512)
    back_second(0)
    back_second(1)
    back_second(2)
    back_second(3)
    for d, h, r in ((1, 0, r_ub1), (3, 64, r_ub3)):
        r0 = ((x - d) % 4) * 128
        landed(out_u.at[rows(r0, 128)], r)
        at = rows(r0 + h, 64)
        go(out_u.at[at], out_u.at[at], peer(dx=d), 14, r_uh, 128)
    back_first(0)
    back_first(1)
    back_first(2)
    back_first(3)
    pass_on(0, 0)
    pass_on(1, 0)
    pass_on(2, 0)
    pass_on(3, 0)
    for k in (1, 3, 2):
        pass_on(0, k)
        pass_on(1, k)
    for k in (1, 3, 2):
        pass_on(2, k)
        pass_on(3, k)
    back_pair(0, 0)
    back_pair(1, 0)
    back_pair(2, 0)
    back_pair(3, 0)
    at = rows((1 - zl) * 512, 512)
    landed(out_q.at[at, mine], r_qbz)
    go(out_q.at[at, mine], out_q.at[at, mine], peer(dc=1), 15, r_qc, 512)
    for d in (1, 3, 2):
        for n in range(4):
            back_pair(n, d)
    landed(out_u.at[0:128], r_uh)
    landed(out_q.at[:, others], r_qc)
    landed(out_r.at[:, others], r_pair)
    left(stat_in, 0)
    for s in sorted(sent):
        if s > 0:
            left(gr.at[0 : sent[s]], s)


KINDS = ("join", "one", "two", "three", "z", "s1", "s2", "s3", "h1", "h3") + tuple(
    f"f{d}_{k}" for d in (1, 3) for k in range(4)
)
SENDS = 16
RECVS = 92


def per_device(user_states, quot_rows, rem_table, neg_rem, pos_quot, pos_rem):
    vmem = pl.BlockSpec(memory_space=pltpu.VMEM)
    hbm = pl.BlockSpec(memory_space=pltpu.HBM)
    return pl.pallas_call(
        kernel,
        out_shape=(
            pltpu.VMEM((NU, D), F32),
            pltpu.VMEM((NN, D), F32),
            pltpu.VMEM((NR, D), F32),
        ),
        in_specs=[hbm] * 6,
        out_specs=(vmem, vmem, vmem),
        scratch_shapes=[
            pltpu.VMEM((NU, D), BF16),
            pltpu.VMEM((NN, D), BF16),
            pltpu.VMEM((NR, D), BF16),
            pltpu.VMEM((1, NN), jnp.int32),
            pltpu.VMEM((1, NU), jnp.int32),
            pltpu.VMEM((1, NU), jnp.int32),
            pltpu.VMEM((NN, D), F32),
            pltpu.VMEM((NN, D), BF16),
            pltpu.VMEM((2, 2, NU, H), F32),
            pltpu.VMEM((2, NU, H), F32),
            pltpu.VMEM((NU, D), F32),
            pltpu.VMEM((NN, NU), F32),
            pltpu.VMEM((NN, NU), BF16),
            pltpu.VMEM((12, 128), F32),
            pltpu.VMEM((15, 12, 128), F32),
            pltpu.VMEM((2, NU), F32),
            pltpu.VMEM((2, NU), F32),
            pltpu.VMEM((8, 128), F32),
            pltpu.VMEM((8, 128), F32),
            pltpu.VMEM((2, NN, H), F32),
            pltpu.VMEM((NN, H), F32),
            pltpu.VMEM((256, NN + 2 * NU), BF16),
            pltpu.VMEM((NN + 2 * NU, D), BF16),
            pltpu.VMEM((2 * NU, D), BF16),
            pltpu.VMEM((NR, H), F32),
            pltpu.VMEM((NN, H), F32),
            pltpu.VMEM((NU, D), F32),
            pltpu.VMEM((128, D), F32),
            pltpu.VMEM((4, 3, 256, H), F32),
            pltpu.VMEM((4, 3, 64, H), F32),
            pltpu.VMEM((4, 7, 8, H), F32),
            pltpu.VMEM((1, 512, H), F32),
            pltpu.VMEM((3, 128, H), F32),
            pltpu.VMEM((6, 128, D), F32),
            pltpu.VMEM((3, 32, D), F32),
            pltpu.SemaphoreType.DMA((6,)),
            pltpu.SemaphoreType.DMA((SENDS,)),
            pltpu.SemaphoreType.DMA((RECVS,)),
        ],
        compiler_params=pltpu.CompilerParams(
            collective_id=0, has_side_effects=True, vmem_limit_bytes=58 << 20
        ),
        cost_estimate=pl.CostEstimate(flops=12 << 30, bytes_accessed=9 << 20, transcendentals=1 << 20),
        name="sampled_softmax_grads",
    )(
        user_states, quot_rows, rem_table,
        neg_rem.reshape(1, NN), pos_quot.reshape(1, NU), pos_rem.reshape(1, NU),
    )


def solution(mesh):
    in_specs = (P("user", None), P("item", None), P(), P("item"), P("user"), P("user"))
    out_specs = (P("user", None), P("item", None), P())
    return jax.shard_map(
        per_device, mesh=mesh, in_specs=in_specs, out_specs=out_specs, check_vma=False
    )
```
